256 devices in a mesh: seq: 64 (over z, y_hi, x), chan: 4 (over y_lo, core).
Axes of the slice: x: 4, y: 4 (y_hi: 2, y_lo: 2; y = y_hi * 2 + y_lo), z: 8, core: 2. Of those that a mesh axis runs over, the one named last changes fastest.
Arguments:
- tokens: bfloat16 [256, 1048576], P('chan', 'seq'), may hold values from -6 to 6
- gate_in: bfloat16 [256, 1048576], P('chan', 'seq'), may hold values from -5 to 5
- gate_out: bfloat16 [256, 1048576], P('chan', 'seq'), may hold values from -5 to 5
- twiddle: float32 [1024, 1024], P('seq'), may hold values from -4 to 4
- first_factor: bfloat16 [1024, 1024], P(('seq', 'chan')), may hold values from -0.1875 to 0.1875
- second_factor: bfloat16 [1024, 1024], P(('seq', 'chan')), may hold values from -0.1875 to 0.1875
- w_up: bfloat16 [4, 64, 128], P('chan'), may hold values from -0.75 to 0.75
- w_down: bfloat16 [4, 128, 64], P('chan'), may hold values from -0.5 to 0.5
- cotangent: bfloat16 [256, 1048576], P('chan', 'seq'), may hold values from -6 to 6
Outputs:
- mixed_out: bfloat16 [256, 1048576], P('chan', 'seq')
- input_grad: bfloat16 [256, 1048576], P('chan', 'seq')
- first_grad: float32 [1024, 1024], P(('seq', 'chan'))
- second_grad: float32 [1024, 1024], P(('seq', 'chan'))
- up_grad: float32 [4, 64, 128], P('chan')
- down_grad: float32 [4, 128, 64], P('chan')
The draws below stay inside these ranges and needn't reach their ends.
All inputs are finite; a program needn't handle non-finite values.
Results may differ from the reference program's by a relative error of at most 0.011.
Values may be sent and summed in bfloat16 or wider, within the bound.
No kernel may reach another device: no remote copies, remote signals or barrier semaphores. Data moves between devices by JAX's collectives and lax.ppermute only.
A program may use at most 128 MiB of HBM per device.

```python
import jax
import jax.numpy as jnp
from jax import lax

N = 1024
CHANNELS = 256
HIDDEN_SIZE = 512
BLOCKS = 4
SEQ_LEN = 1048576


def shard_levels(rng, dims, cuts, least, high):
    gain, own = 1.0, jax.random.fold_in(rng, 6)
    for axis_at, shards_of in cuts:
        draws = jnp.exp(jax.random.uniform(jax.random.fold_in(own, axis_at), (shards_of,), jnp.float32, least / len(cuts), high / len(cuts)))
        gain = gain * jnp.repeat(draws, dims[axis_at] // shards_of).reshape([-1 if axis == axis_at else 1 for axis in range(len(dims))])
    return gain


def centred(key, shape, width, bound, cuts=(), held_as=jnp.bfloat16):
    array = width * jax.random.normal(key, shape, jnp.float32)
    if cuts:
        array = array * shard_levels(key, shape, cuts, -0.22, 0.18)
    return jnp.clip(array, -bound, bound).astype(held_as)


def setup_inputs(seed: int = 0) -> dict:
    arg_keys = jax.random.split(jax.random.key(seed), 10)
    tokens = centred(arg_keys[0], (CHANNELS, SEQ_LEN), 1.0, 6.0, ((0, 4), (1, 64)))
    gate_in = centred(arg_keys[1], (CHANNELS, SEQ_LEN), 1.0, 5.0, ((0, 4), (1, 64)))
    gate_out = centred(arg_keys[2], (CHANNELS, SEQ_LEN), 1.0, 5.0, ((0, 4), (1, 64)))
    twiddle = centred(arg_keys[3], (N, N), 1.0, 4.0, ((0, 64),), jnp.float32)
    first_factor = centred(arg_keys[4], (N, N), N ** -0.5, 0.1875, ((0, 256),))
    second_factor = centred(arg_keys[5], (N, N), N ** -0.5, 0.1875, ((0, 256),))
    w_up = centred(arg_keys[6], (BLOCKS, CHANNELS // BLOCKS, HIDDEN_SIZE // BLOCKS), (CHANNELS // BLOCKS) ** -0.5, 0.75, ((0, 4),))
    w_down = centred(arg_keys[7], (BLOCKS, HIDDEN_SIZE // BLOCKS, CHANNELS // BLOCKS), (HIDDEN_SIZE // BLOCKS) ** -0.5, 0.5, ((0, 4),))
    cotangent = centred(arg_keys[8], (CHANNELS, SEQ_LEN), 1.0, 6.0, ((0, 4), (1, 64)))
    return dict(tokens=tokens, gate_in=gate_in, gate_out=gate_out, twiddle=twiddle, first_factor=first_factor, second_factor=second_factor, w_up=w_up, w_down=w_down, cotangent=cotangent)


def gelu_value(values):
    return 0.5 * values * (1.0 + lax.erf(values * 0.7071067811865476))


def gelu_slope(values):
    cumulative = 0.5 * (1.0 + lax.erf(values * 0.7071067811865476))
    density = jnp.exp(-0.5 * values * values) * 0.3989422804014327
    return cumulative + values * density


def reference(tokens, gate_in, gate_out, twiddle, first_factor, second_factor, w_up, w_down, cotangent):
    tokens = tokens.T
    gate_in = gate_in.T
    gate_out = gate_out.T
    cotangent = cotangent.T
    chan_block = CHANNELS // BLOCKS
    hid_block = HIDDEN_SIZE // BLOCKS
    sub_width = hid_block // BLOCKS
    first_wide = first_factor.astype(jnp.float32)
    second_wide = second_factor.astype(jnp.float32)
    gated = (tokens.astype(jnp.float32) * gate_in.astype(jnp.float32)).astype(jnp.bfloat16)
    gated_cube = gated.reshape(N, N, CHANNELS).astype(jnp.float32)
    segment_one = (jnp.einsum("kb,abc->akc", first_wide, gated_cube) * twiddle[:, :, None]).astype(jnp.bfloat16)
    segment_wide = segment_one.astype(jnp.float32)
    product = jnp.einsum("ja,akc->kjc", second_wide, segment_wide).reshape(SEQ_LEN, CHANNELS)
    mixer = (product * gate_out.astype(jnp.float32)).astype(jnp.bfloat16)
    mixer_blocks = mixer.reshape(SEQ_LEN, BLOCKS, chan_block).astype(jnp.float32)
    hidden = jnp.einsum("tgi,gih->tgh", mixer_blocks, w_up.astype(jnp.float32))
    activated = gelu_value(hidden).astype(jnp.bfloat16)
    permuted = jnp.transpose(activated.reshape(SEQ_LEN, BLOCKS, BLOCKS, sub_width), (0, 2, 1, 3)).reshape(SEQ_LEN, BLOCKS, hid_block)
    down_part = jnp.einsum("trh,rho->tro", permuted.astype(jnp.float32), w_down.astype(jnp.float32))
    mixed_out = (mixer_blocks + down_part).astype(jnp.bfloat16).reshape(SEQ_LEN, CHANNELS)
    cot_blocks = cotangent.reshape(SEQ_LEN, BLOCKS, chan_block).astype(jnp.float32)
    permuted_grad = jnp.einsum("tro,rho->trh", cot_blocks, w_down.astype(jnp.float32)).astype(jnp.bfloat16)
    down_grad = jnp.einsum("trh,tro->rho", permuted.astype(jnp.float32), cot_blocks)
    act_grad = jnp.transpose(permuted_grad.reshape(SEQ_LEN, BLOCKS, BLOCKS, sub_width), (0, 2, 1, 3)).reshape(SEQ_LEN, BLOCKS, hid_block)
    hidden_grad = (act_grad.astype(jnp.float32) * gelu_slope(hidden)).astype(jnp.bfloat16)
    hidden_wide = hidden_grad.astype(jnp.float32)
    up_grad = jnp.einsum("tgi,tgh->gih", mixer_blocks, hidden_wide)
    mixer_grad = cot_blocks + jnp.einsum("tgh,gih->tgi", hidden_wide, w_up.astype(jnp.float32))
    weighted = (mixer_grad.reshape(SEQ_LEN, CHANNELS) * gate_out.astype(jnp.float32)).astype(jnp.bfloat16)
    weighted_cube = weighted.reshape(N, N, CHANNELS).astype(jnp.float32)
    second_grad = jnp.einsum("kjc,akc->ja", weighted_cube, segment_wide)
    back_one = jnp.einsum("ja,kjc->akc", second_wide, weighted_cube).astype(jnp.bfloat16)
    shifted = (back_one.astype(jnp.float32) * twiddle[:, :, None]).astype(jnp.bfloat16)
    shifted_wide = shifted.astype(jnp.float32)
    first_grad = jnp.einsum("akc,abc->kb", shifted_wide, gated_cube)
    spread = jnp.einsum("kb,akc->abc", first_wide, shifted_wide).reshape(SEQ_LEN, CHANNELS)
    input_grad = (spread * gate_in.astype(jnp.float32)).astype(jnp.bfloat16)
    return mixed_out.T, input_grad.T, first_grad, second_grad, up_grad, down_grad
```

```python
import functools

import jax
import jax.numpy as jnp
import numpy as np
from jax import lax
from jax.experimental import pallas as pl
from jax.experimental.pallas import tpu as pltpu
from jax.sharding import Mesh
from jax.sharding import PartitionSpec as P

AXES = ("z", "yh", "x", "yl", "core")
SIZES = (8, 2, 4, 2, 2)
SEQ = ("z", "yh", "x")
CHAN = ("yl", "core")
PLANE = ("yh", "x", "yl")
F32 = jnp.float32
BF16 = jnp.bfloat16
MIB = 1024 * 1024


def params(mib, **kw):
    return pltpu.CompilerParams(vmem_limit_bytes=mib * MIB, **kw)


def cost(us, flops=0):
    return pl.CostEstimate(flops=flops, bytes_accessed=int(us * 3.0e6), transcendentals=0)


def full(shape):
    return pl.BlockSpec(shape, lambda i: (0,) * len(shape))


def nt(a, b):
    return lax.dot_general(a, b, (((1,), (1,)), ((), ())), preferred_element_type=F32)


def nn(a, b):
    return lax.dot_general(a, b, (((1,), (0,)), ((), ())), preferred_element_type=F32)


def tn(a, b):
    return lax.dot_general(a, b, (((0,), (0,)), ((), ())), preferred_element_type=F32)


def prep_kernel(tok_ref, gate_ref, cot_ref, wd_ref, rows_ref, *grad_refs):
    rows_ref[...] = (tok_ref[...].astype(F32) * gate_ref[...].astype(F32)).astype(BF16)
    grad = nn(wd_ref[...], cot_ref[...]).astype(BF16)
    for i, ref in enumerate(grad_refs):
        ref[...] = grad[i * 32 : (i + 1) * 32]


def prep(tokens, gate_in, cotangent, wd):
    chan, positions = tokens.shape
    blocks = positions // 1024
    cols = pl.BlockSpec((chan, 1024), lambda i: (0, i))
    part = pl.BlockSpec((32, 1024), lambda i: (0, i))
    return pl.pallas_call(
        prep_kernel,
        grid=(blocks,),
        in_specs=[cols, cols, cols, full(wd.shape)],
        out_specs=[pl.BlockSpec((chan, 1024), lambda i: (i, 0))] + [part] * 4,
        out_shape=[jax.ShapeDtypeStruct((blocks * chan, 1024), BF16)]
        + [jax.ShapeDtypeStruct((32, positions), BF16)] * 4,
        compiler_params=params(32),
        cost_estimate=cost(5),
        name="prep",
    )(tokens, gate_in, cotangent, wd)


def assemble_kernel(table_ref, own_ref, other_ref, out_ref):
    first = table_ref[16] == 0
    for m in range(16):
        at = table_ref[m]
        own, other = own_ref[at], other_ref[at]
        out_ref[:, m, :, :512] = jnp.where(first, own, other)
        out_ref[:, m, :, 512:] = jnp.where(first, other, own)


def assemble(own, other, table):
    out = pl.pallas_call(
        assemble_kernel,
        in_specs=[pl.BlockSpec(memory_space=pltpu.SMEM)] + [pl.BlockSpec(memory_space=pltpu.VMEM)] * 2,
        out_specs=pl.BlockSpec(memory_space=pltpu.VMEM),
        out_shape=jax.ShapeDtypeStruct((8, 16, 8, 1024), BF16),
        compiler_params=params(32),
        cost_estimate=cost(3),
        name="assemble",
    )(table, own, other)
    return out.reshape(1024, 1024)


def spread_twiddle(tw):
    high = tw.astype(BF16)
    rest = tw - high.astype(F32)
    mid = rest.astype(BF16)
    low = (rest - mid.astype(F32)).astype(BF16)
    terms = jnp.concatenate([high, mid, low], axis=0)
    row = lax.broadcasted_iota(jnp.int32, (48, 1024), 0)
    lane = lax.broadcasted_iota(jnp.int32, (48, 1024), 1)
    pick = jnp.where(row % 16 == lane // 64, 1.0, 0.0).astype(BF16)
    return tn(terms, pick)


def segment_kernel(first_ref, rows_ref, tw_ref, out_ref):
    scale = spread_twiddle(tw_ref[...])
    out_ref[...] = (nt(first_ref[...], rows_ref[...]) * scale).astype(BF16)


def segment(first, rows, tw):
    return pl.pallas_call(
        segment_kernel,
        grid=(4,),
        in_specs=[
            pl.BlockSpec((256, 1024), lambda i: (i, 0)),
            full((1024, 1024)),
            pl.BlockSpec((16, 256), lambda i: (0, i)),
        ],
        out_specs=pl.BlockSpec((256, 1024), lambda i: (i, 0)),
        out_shape=jax.ShapeDtypeStruct((1024, 1024), BF16),
        compiler_params=params(32),
        cost_estimate=cost(6),
        name="segment",
    )(first, rows, tw)


def swap_lanes(values):
    return pltpu.roll(values, 64, 1)


def middle_kernel(
    moved_ref, second_ref, gate_ref, cot_ref, g0, g1, g2, g3, wu_ref,
    back_ref, left_ref, weighted_ref, mixer_ref, a0, a1, a2, a3, up_ref,
    wide_ref, prod_ref,
):
    step = pl.program_id(0)
    grads, acts = (g0, g1, g2, g3), (a0, a1, a2, a3)

    @pl.when(step == 0)
    def _():
        for p in range(8):
            wide_ref[p * 1024 : (p + 1) * 1024] = moved_ref[:, p * 128 : (p + 1) * 128].astype(F32)
        up_ref[...] = jnp.zeros_like(up_ref)

    low = lax.broadcasted_iota(jnp.int32, (64, 128), 1) < 64
    for pair in range(2):
        k = step * 4 + pair * 2
        for p in range(8):
            lanes = slice(p * 128, (p + 1) * 128)
            one = wide_ref[pl.ds(p * 1024 + k, 64, stride=16)]
            two = wide_ref[pl.ds(p * 1024 + k + 1, 64, stride=16)]
            both = jnp.concatenate(
                [jnp.where(low, one, swap_lanes(two)), jnp.where(low, swap_lanes(one), two)], axis=0
            )
            left_ref[pair * 128 : (pair + 1) * 128, lanes] = both.T.astype(BF16)
    prod_ref[...] = nt(left_ref[...], second_ref[...])
    wu = wu_ref[...]
    width = 256
    up = jnp.zeros((64, 128), F32)
    for kk in range(4):
        for t in range(0, 1024, width):
            at = slice(kk * 1024 + t, kk * 1024 + t + width)
            gate = gate_ref[:, at].astype(F32)
            mix = (prod_ref[kk * 64 : (kk + 1) * 64, t : t + width] * gate).astype(BF16)
            mixer_ref[:, at] = mix
            hidden = tn(wu, mix)
            cum = 0.5 * (1.0 + lax.erf(hidden * 0.7071067811865476))
            act = (hidden * cum).astype(BF16)
            slope = cum + hidden * (jnp.exp(-0.5 * hidden * hidden) * 0.3989422804014327)
            for i in range(4):
                acts[i][:, at] = act[i * 32 : (i + 1) * 32]
            grad = jnp.concatenate([g[:, at] for g in grads], axis=0)
            hgrad = (grad.astype(F32) * slope).astype(BF16)
            up += nt(mix, hgrad)
            mgrad = cot_ref[:, at].astype(F32) + nn(wu, hgrad)
            weighted_ref[kk * 64 : (kk + 1) * 64, t : t + width] = (mgrad * gate).astype(BF16)
    up_ref[...] += up
    prod_ref[...] = nn(weighted_ref[...], second_ref[...])
    for pair in range(2):
        k = step * 4 + pair * 2
        for p in range(8):
            lanes = slice(p * 128, (p + 1) * 128)
            both = prod_ref[pair * 128 : (pair + 1) * 128, lanes].T
            top, bottom = both[:64], both[64:]
            wide_ref[pl.ds(p * 1024 + k, 64, stride=16)] = jnp.where(low, top, swap_lanes(bottom))
            wide_ref[pl.ds(p * 1024 + k + 1, 64, stride=16)] = jnp.where(low, swap_lanes(top), bottom)

    @pl.when(step == 3)
    def _():
        for p in range(8):
            back_ref[:, p * 128 : (p + 1) * 128] = wide_ref[p * 1024 : (p + 1) * 1024].astype(BF16)


def middle(moved, second, gate_out, cotangent, grads, wu):
    chan, positions = gate_out.shape
    cols = pl.BlockSpec((chan, 4096), lambda i: (0, i))
    part = pl.BlockSpec((32, 4096), lambda i: (0, i))
    square = full((1024, 1024))
    rows = pl.BlockSpec((256, 1024), lambda i: (i, 0))
    big = jax.ShapeDtypeStruct((1024, 1024), BF16)
    small = jax.ShapeDtypeStruct((32, positions), BF16)
    return pl.pallas_call(
        middle_kernel,
        grid=(4,),
        in_specs=[square, square, cols, cols] + [part] * 4 + [full(wu.shape)],
        out_specs=[square, rows, rows, cols] + [part] * 4 + [full((64, 128))],
        out_shape=[big, big, big, jax.ShapeDtypeStruct((chan, positions), BF16)]
        + [small] * 4
        + [jax.ShapeDtypeStruct((64, 128), F32)],
        scratch_shapes=[pltpu.VMEM((8192, 128), F32), pltpu.VMEM((256, 1024), F32)],
        compiler_params=params(48),
        cost_estimate=cost(25),
        name="middle",
    )(moved, second, gate_out, cotangent, *grads, wu)


def split_columns(first, total, send_ref, keep_ref):
    for z in range(8):
        part = total[z * 128 : (z + 1) * 128].reshape(16, 8, 1024)
        lo, hi = part[:, :, :512], part[:, :, 512:]
        send_ref[:, z] = jnp.where(first, hi, lo).astype(BF16)
        keep_ref[:, z] = jnp.where(first, lo, hi)


def second_kernel(core_ref, weighted_ref, left_ref, send_ref, keep_ref):
    split_columns(core_ref[0] == 0, tn(weighted_ref[...], left_ref[...]), send_ref, keep_ref)


HALF = [
    jax.ShapeDtypeStruct((16, 8, 8, 512), BF16),
    jax.ShapeDtypeStruct((16, 8, 8, 512), F32),
]


def second_part(core, weighted, left):
    vmem = pl.BlockSpec(memory_space=pltpu.VMEM)
    return pl.pallas_call(
        second_kernel,
        in_specs=[pl.BlockSpec(memory_space=pltpu.SMEM), vmem, vmem],
        out_specs=[vmem, vmem],
        out_shape=HALF,
        compiler_params=params(40),
        cost_estimate=cost(7),
        name="second_part",
    )(core, weighted, left)


def first_kernel(core_ref, back_ref, rows_ref, tw_ref, send_ref, keep_ref, shifted_ref):
    for i in range(4):
        at = slice(i * 256, (i + 1) * 256)
        scale = spread_twiddle(tw_ref[:, at])
        shifted_ref[at] = (back_ref[at].astype(F32) * scale).astype(BF16)
    split_columns(core_ref[0] == 0, nn(shifted_ref[...], rows_ref[...]), send_ref, keep_ref)


def first_part(core, back, rows, tw):
    vmem = pl.BlockSpec(memory_space=pltpu.VMEM)
    return pl.pallas_call(
        first_kernel,
        in_specs=[pl.BlockSpec(memory_space=pltpu.SMEM), vmem, vmem, vmem],
        out_specs=[vmem, vmem, vmem],
        out_shape=HALF + [jax.ShapeDtypeStruct((1024, 1024), BF16)],
        compiler_params=params(40),
        cost_estimate=cost(7),
        name="first_part",
    )(core, back, rows, tw)


def input_kernel(shifted_ref, first_ref, gate_ref, out_ref):
    spread = tn(shifted_ref[...], first_ref[...])
    for q in range(4):
        at = slice(q * 1024, (q + 1) * 1024)
        out_ref[:, at] = (spread[q * 64 : (q + 1) * 64] * gate_ref[:, at].astype(F32)).astype(BF16)


def input_part(shifted, first, gate_in):
    cols = pl.BlockSpec((64, 4096), lambda i: (0, i))
    return pl.pallas_call(
        input_kernel,
        grid=(4,),
        in_specs=[pl.BlockSpec((1024, 256), lambda i: (0, i)), full((1024, 1024)), cols],
        out_specs=cols,
        out_shape=jax.ShapeDtypeStruct(gate_in.shape, BF16),
        compiler_params=params(32),
        cost_estimate=cost(7),
        name="input_part",
    )(shifted, first, gate_in)


def output_kernel(mixer_ref, p0, p1, p2, p3, cot_ref, wd_ref, out_ref, down_ref):
    @pl.when(pl.program_id(0) == 0)
    def _():
        down_ref[...] = jnp.zeros_like(down_ref)

    permuted = jnp.concatenate([p[...] for p in (p0, p1, p2, p3)], axis=0)
    out_ref[...] = (mixer_ref[...].astype(F32) + tn(wd_ref[...], permuted)).astype(BF16)
    down_ref[...] += nt(permuted, cot_ref[...])


def output_part(mixer, parts, cotangent, wd):
    cols = pl.BlockSpec((64, 4096), lambda i: (0, i))
    part = pl.BlockSpec((32, 4096), lambda i: (0, i))
    return pl.pallas_call(
        output_kernel,
        grid=(4,),
        in_specs=[cols] + [part] * 4 + [cols, full(wd.shape)],
        out_specs=[cols, full((128, 64))],
        out_shape=[jax.ShapeDtypeStruct(mixer.shape, BF16), jax.ShapeDtypeStruct((128, 64), F32)],
        compiler_params=params(32),
        cost_estimate=cost(8),
        name="output_part",
    )(mixer, *parts, cotangent, wd)


def swap(values, axis, bit):
    size = int(np.prod([SIZES[AXES.index(a)] for a in ((axis,) if isinstance(axis, str) else axis)]))
    return lax.ppermute(values, axis, [(i, i ^ bit) for i in range(size)])


def copies(values, count):
    return jnp.broadcast_to(values[None], (count,) + values.shape)


def chan_swap(parts):
    return [parts[0]] + [swap(parts[i], CHAN, i) for i in (1, 2, 3)]


def gather_factors(first, second, core):
    both = jnp.stack([first, second]).reshape(2, 4, 2, 512)
    mine = lax.dynamic_index_in_dim(both, core, 2, keepdims=False)
    theirs = lax.dynamic_index_in_dim(both, 1 - core, 2, keepdims=False)
    theirs = swap(theirs, "core", 1)
    rows = jnp.where(
        core == 0,
        jnp.concatenate([mine, theirs], axis=1),
        jnp.concatenate([theirs, mine], axis=1),
    )
    column = lax.all_to_all(copies(rows, 8), "z", 0, 0, tiled=True)
    plane = lax.all_to_all(copies(column, 16), PLANE, 0, 0, tiled=True)
    return plane[:, :, 0], plane[:, :, 1]


def scatter_sum(send, keep, core):
    total = (keep + swap(send, "core", 1).astype(F32)).astype(BF16)
    grads = total.shape[0]
    total = lax.all_to_all(jnp.swapaxes(total, 0, 1), PLANE, 0, 0, tiled=True)
    total = jnp.sum(total.astype(F32), axis=0)
    total = lax.all_to_all(jnp.swapaxes(total, 0, 1), "z", 0, 0, tiled=True)
    total = jnp.sum(total, axis=0).reshape(grads, 2, 4, 512)
    mine = lax.dynamic_index_in_dim(total, core, 1, keepdims=False)
    theirs = swap(lax.dynamic_index_in_dim(total, 1 - core, 1, keepdims=False), "core", 1)
    return jnp.where(
        core == 0,
        jnp.concatenate([mine, theirs], axis=2),
        jnp.concatenate([theirs, mine], axis=2),
    )


def local(tokens, gate_in, gate_out, twiddle, first_factor, second_factor, w_up, w_down, cotangent):
    core = lax.axis_index("core")
    chan = lax.axis_index(CHAN)
    order = chan ^ jnp.arange(4, dtype=jnp.int32)
    core_word = core.astype(jnp.int32).reshape(1)
    table = jnp.concatenate([jnp.arange(16, dtype=jnp.int32), core_word])
    wd = w_down[0].reshape(4, 32, 64)[order].reshape(128, 64)
    wu = w_up[0].reshape(64, 4, 32)[:, order].reshape(64, 128)

    second_turned = jnp.swapaxes(second_factor.reshape(4, 64, 16), 1, 2).reshape(4, 1024)
    first_half, second_half = gather_factors(first_factor, second_turned, core)
    rows, *grads = prep(tokens, gate_in, cotangent, wd)
    first = assemble(first_half, swap(first_half, "core", 1), table)
    seg = segment(first, rows, twiddle)
    moved = lax.all_to_all(seg.reshape(64, 16, 1024), SEQ, 0, 0, tiled=True).reshape(1024, 1024)
    grads = chan_swap(grads)
    second = assemble(second_half, swap(second_half, "core", 1), table)
    back, left, weighted, mixer, *rest = middle(moved, second, gate_out, cotangent, grads, wu)
    acts, up = rest[:4], rest[4]
    returned = lax.all_to_all(back.reshape(64, 16, 1024), SEQ, 0, 0, tiled=True).reshape(1024, 1024)
    acts = chan_swap(acts)
    second_send, second_keep = second_part(core_word, weighted, left)
    mixed_out, down = output_part(mixer, acts, cotangent, wd)
    first_send, first_keep, shifted = first_part(core_word, returned, rows, twiddle)
    both = scatter_sum(
        jnp.stack([first_send, second_send]), jnp.stack([first_keep, second_keep]), core
    )
    input_grad = input_part(shifted, first, gate_in)
    first_grad = both[0]
    second_grad = jnp.swapaxes(both[1].reshape(4, 16, 64), 1, 2).reshape(4, 1024)
    up = up.reshape(64, 4, 32)[:, order].reshape(64, 128)
    down = down.reshape(4, 32, 64)[order].reshape(128, 64)
    small = jnp.concatenate([up, down.reshape(64, 128)], axis=0)
    for axis, bit in (("x", 1), ("x", 2), ("yh", 1), ("z", 1), ("z", 2), ("z", 4)):
        small = small + swap(small, axis, bit)
    return (
        mixed_out,
        input_grad,
        first_grad,
        second_grad,
        small[:64][None],
        small[64:].reshape(1, 128, 64),
    )


def solution(mesh):
    fine = Mesh(mesh.devices.reshape(SIZES), AXES)
    wide = P(CHAN, SEQ)
    factor = P(AXES, None)
    weight = P(CHAN, None, None)
    return jax.shard_map(
        local,
        mesh=fine,
        in_specs=(wide, wide, wide, P(SEQ, None), factor, factor, weight, weight, wide),
        out_specs=(wide, wide, factor, factor, weight, weight),
        check_vma=False,
    )
```

```python
import functools

import jax
import jax.numpy as jnp
import numpy as np
from jax import lax
from jax.experimental import pallas as pl
from jax.experimental.pallas import tpu as pltpu
from jax.sharding import Mesh
from jax.sharding import PartitionSpec as P

AXES = ("z", "yh", "x", "yl", "core")
SIZES = (8, 2, 4, 2, 2)
SEQ = ("z", "yh", "x")
CHAN = ("yl", "core")
PLANE = ("yh", "x", "yl")
F32 = jnp.float32
BF16 = jnp.bfloat16
MIB = 1024 * 1024


def params(mib, **kw):
    return pltpu.CompilerParams(vmem_limit_bytes=mib * MIB, **kw)


def cost(us, flops=0):
    return pl.CostEstimate(flops=flops, bytes_accessed=int(us * 3.0e3), transcendentals=0)


def full(shape):
    return pl.BlockSpec(shape, lambda i: (0,) * len(shape))


def nt(a, b):
    return lax.dot_general(a, b, (((1,), (1,)), ((), ())), preferred_element_type=F32)


def nn(a, b):
    return lax.dot_general(a, b, (((1,), (0,)), ((), ())), preferred_element_type=F32)


def tn(a, b):
    return lax.dot_general(a, b, (((0,), (0,)), ((), ())), preferred_element_type=F32)


def grads_kernel(cot_ref, wd_ref, *grad_refs):
    grad = nn(wd_ref[...], cot_ref[...]).astype(BF16)
    for i, ref in enumerate(grad_refs):
        ref[...] = grad[i * 32 : (i + 1) * 32]


def grads_part(cotangent, wd):
    chan, positions = cotangent.shape
    part = pl.BlockSpec((32, 4096), lambda i: (0, i))
    return pl.pallas_call(
        grads_kernel,
        grid=(positions // 4096,),
        in_specs=[pl.BlockSpec((chan, 4096), lambda i: (0, i)), full(wd.shape)],
        out_specs=[part] * 4,
        out_shape=[jax.ShapeDtypeStruct((32, positions), BF16)] * 4,
        compiler_params=params(60),
        cost_estimate=cost(4),
        name="grads_part",
    )(cotangent, wd)


def gated_kernel(tok_ref, gate_ref, rows_ref):
    for q in range(4):
        at = slice(q * 1024, (q + 1) * 1024)
        rows_ref[q * 64 : (q + 1) * 64] = (
            tok_ref[:, at].astype(F32) * gate_ref[:, at].astype(F32)
        ).astype(BF16)


def gated_part(tokens, gate_in):
    cols = pl.BlockSpec((64, 4096), lambda i: (0, i))
    return pl.pallas_call(
        gated_kernel,
        grid=(4,),
        in_specs=[cols, cols],
        out_specs=pl.BlockSpec((256, 1024), lambda i: (i, 0)),
        out_shape=jax.ShapeDtypeStruct((1024, 1024), BF16),
        compiler_params=params(60),
        cost_estimate=cost(4),
        name="gated_part",
    )(tokens, gate_in)


def assemble_kernel(table_ref, own_ref, other_ref, out_ref):
    first = table_ref[16] == 0
    for m in range(16):
        at = table_ref[m]
        own, other = own_ref[at], other_ref[at]
        out_ref[:, m, :, :512] = jnp.where(first, own, other)
        out_ref[:, m, :, 512:] = jnp.where(first, other, own)


def assemble(own, other, table):
    out = pl.pallas_call(
        assemble_kernel,
        in_specs=[pl.BlockSpec(memory_space=pltpu.SMEM)] + [pl.BlockSpec(memory_space=pltpu.VMEM)] * 2,
        out_specs=pl.BlockSpec(memory_space=pltpu.VMEM),
        out_shape=jax.ShapeDtypeStruct((8, 16, 8, 1024), BF16),
        compiler_params=params(60),
        cost_estimate=cost(3),
        name="assemble",
    )(table, own, other)
    return out.reshape(1024, 1024)


def fan_kernel(column_ref, *refs):
    for m in range(refs[-1].shape[0]):
        refs[-1][m] = column_ref[...]


def fan(column, count, after):
    vmem = pl.BlockSpec(memory_space=pltpu.VMEM)
    return pl.pallas_call(
        fan_kernel,
        in_specs=[vmem] + [pl.BlockSpec(memory_space=pl.ANY)] * len(after),
        out_specs=vmem,
        out_shape=jax.ShapeDtypeStruct((count,) + column.shape, BF16),
        compiler_params=params(60),
        cost_estimate=cost(1),
        name="fan",
    )(column, *after)


def spread_twiddle(tw):
    high = tw.astype(BF16)
    rest = tw - high.astype(F32)
    mid = rest.astype(BF16)
    low = (rest - mid.astype(F32)).astype(BF16)
    terms = jnp.concatenate([high, mid, low], axis=0)
    row = lax.broadcasted_iota(jnp.int32, (48, 1024), 0)
    lane = lax.broadcasted_iota(jnp.int32, (48, 1024), 1)
    pick = jnp.where(row % 16 == lane // 64, 1.0, 0.0).astype(BF16)
    return tn(terms, pick)


def segment_kernel(first_ref, rows_ref, tw_ref, out_ref):
    scale = spread_twiddle(tw_ref[...])
    out_ref[...] = (nt(first_ref[...], rows_ref[...]) * scale).astype(BF16)


def segment(first, rows, tw):
    return pl.pallas_call(
        segment_kernel,
        grid=(4,),
        in_specs=[
            pl.BlockSpec((256, 1024), lambda i: (i, 0)),
            full((1024, 1024)),
            pl.BlockSpec((16, 256), lambda i: (0, i)),
        ],
        out_specs=pl.BlockSpec((256, 1024), lambda i: (i, 0)),
        out_shape=jax.ShapeDtypeStruct((1024, 1024), BF16),
        compiler_params=params(60),
        cost_estimate=cost(6),
        name="segment",
    )(first, rows, tw)


def swap_lanes(values):
    return pltpu.roll(values, 64, 1)


def middle_kernel(
    moved_ref, second_ref, gate_ref, cot_ref, g0, g1, g2, g3, wu_ref,
    back_ref, left_ref, weighted_ref, mixer_ref, a0, a1, a2, a3, up_ref,
    wide_ref, prod_ref,
):
    step = pl.program_id(0)
    grads, acts = (g0, g1, g2, g3), (a0, a1, a2, a3)

    @pl.when(step == 0)
    def _():
        for p in range(8):
            wide_ref[p * 1024 : (p + 1) * 1024] = moved_ref[:, p * 128 : (p + 1) * 128].astype(F32)
        up_ref[...] = jnp.zeros_like(up_ref)

    low = lax.broadcasted_iota(jnp.int32, (64, 128), 1) < 64
    for pair in range(2):
        k = step * 4 + pair * 2
        for p in range(8):
            lanes = slice(p * 128, (p + 1) * 128)
            one = wide_ref[pl.ds(p * 1024 + k, 64, stride=16)]
            two = wide_ref[pl.ds(p * 1024 + k + 1, 64, stride=16)]
            both = jnp.concatenate(
                [jnp.where(low, one, swap_lanes(two)), jnp.where(low, swap_lanes(one), two)], axis=0
            )
            left_ref[pair * 128 : (pair + 1) * 128, lanes] = both.T.astype(BF16)
    prod_ref[...] = nt(left_ref[...], second_ref[...])
    wu = wu_ref[...]
    width = 256
    up = jnp.zeros((64, 128), F32)
    for kk in range(4):
        for t in range(0, 1024, width):
            at = slice(kk * 1024 + t, kk * 1024 + t + width)
            gate = gate_ref[:, at].astype(F32)
            mix = (prod_ref[kk * 64 : (kk + 1) * 64, t : t + width] * gate).astype(BF16)
            mixer_ref[:, at] = mix
            hidden = tn(wu, mix)
            cum = 0.5 * (1.0 + lax.erf(hidden * 0.7071067811865476))
            act = (hidden * cum).astype(BF16)
            slope = cum + hidden * (jnp.exp(-0.5 * hidden * hidden) * 0.3989422804014327)
            for i in range(4):
                acts[i][:, at] = act[i * 32 : (i + 1) * 32]
            grad = jnp.concatenate([g[:, at] for g in grads], axis=0)
            hgrad = (grad.astype(F32) * slope).astype(BF16)
            up += nt(mix, hgrad)
            mgrad = cot_ref[:, at].astype(F32) + nn(wu, hgrad)
            weighted_ref[kk * 64 : (kk + 1) * 64, t : t + width] = (mgrad * gate).astype(BF16)
    up_ref[...] += up
    prod_ref[...] = nn(weighted_ref[...], second_ref[...])
    for pair in range(2):
        k = step * 4 + pair * 2
        for p in range(8):
            lanes = slice(p * 128, (p + 1) * 128)
            both = prod_ref[pair * 128 : (pair + 1) * 128, lanes].T
            top, bottom = both[:64], both[64:]
            wide_ref[pl.ds(p * 1024 + k, 64, stride=16)] = jnp.where(low, top, swap_lanes(bottom))
            wide_ref[pl.ds(p * 1024 + k + 1, 64, stride=16)] = jnp.where(low, swap_lanes(top), bottom)

    @pl.when(step == 3)
    def _():
        for p in range(8):
            back_ref[:, p * 128 : (p + 1) * 128] = wide_ref[p * 1024 : (p + 1) * 1024].astype(BF16)


def middle(moved, second, gate_out, cotangent, grads, wu):
    chan, positions = gate_out.shape
    cols = pl.BlockSpec((chan, 4096), lambda i: (0, i))
    part = pl.BlockSpec((32, 4096), lambda i: (0, i))
    square = full((1024, 1024))
    rows = pl.BlockSpec((256, 1024), lambda i: (i, 0))
    big = jax.ShapeDtypeStruct((1024, 1024), BF16)
    small = jax.ShapeDtypeStruct((32, positions), BF16)
    return pl.pallas_call(
        middle_kernel,
        grid=(4,),
        in_specs=[square, square, cols, cols] + [part] * 4 + [full(wu.shape)],
        out_specs=[square, rows, rows, cols] + [part] * 4 + [full((64, 128))],
        out_shape=[big, big, big, jax.ShapeDtypeStruct((chan, positions), BF16)]
        + [small] * 4
        + [jax.ShapeDtypeStruct((64, 128), F32)],
        scratch_shapes=[pltpu.VMEM((8192, 128), F32), pltpu.VMEM((256, 1024), F32)],
        compiler_params=params(60),
        cost_estimate=cost(25),
        name="middle",
    )(moved, second, gate_out, cotangent, *grads, wu)


def split_columns(table_ref, total, send_ref, keep_ref):
    first = table_ref[16] == 0
    for m in range(16):
        at = table_ref[m]
        for z in range(8):
            row = z * 128 + m * 8
            lo, hi = total[row : row + 8, :512], total[row : row + 8, 512:]
            send_ref[at, z] = jnp.where(first, hi, lo).astype(BF16)
            keep_ref[at, z] = jnp.where(first, lo, hi)


def second_kernel(table_ref, weighted_ref, left_ref, send_ref, keep_ref, total_ref):
    total_ref[...] = tn(weighted_ref[...], left_ref[...])
    split_columns(table_ref, total_ref, send_ref, keep_ref)


HALF = [
    jax.ShapeDtypeStruct((16, 8, 8, 512), BF16),
    jax.ShapeDtypeStruct((16, 8, 8, 512), F32),
]


def second_part(table, weighted, left):
    vmem = pl.BlockSpec(memory_space=pltpu.VMEM)
    return pl.pallas_call(
        second_kernel,
        in_specs=[pl.BlockSpec(memory_space=pltpu.SMEM), vmem, vmem],
        out_specs=[vmem, vmem],
        out_shape=HALF,
        scratch_shapes=[pltpu.VMEM((1024, 1024), F32)],
        compiler_params=params(60),
        cost_estimate=cost(7),
        name="second_part",
    )(table, weighted, left)


def first_kernel(table_ref, back_ref, rows_ref, tw_ref, *refs):
    send_ref, keep_ref, shifted_ref, total_ref = refs[-4:]
    for i in range(4):
        at = slice(i * 256, (i + 1) * 256)
        scale = spread_twiddle(tw_ref[:, at])
        shifted_ref[at] = (back_ref[at].astype(F32) * scale).astype(BF16)
    total_ref[...] = nn(shifted_ref[...], rows_ref[...])
    split_columns(table_ref, total_ref, send_ref, keep_ref)


def first_part(table, back, rows, tw, after):
    vmem = pl.BlockSpec(memory_space=pltpu.VMEM)
    return pl.pallas_call(
        first_kernel,
        in_specs=[pl.BlockSpec(memory_space=pltpu.SMEM), vmem, vmem, vmem]
        + [pl.BlockSpec(memory_space=pl.ANY)] * len(after),
        out_specs=[vmem, vmem, vmem],
        out_shape=HALF + [jax.ShapeDtypeStruct((1024, 1024), BF16)],
        scratch_shapes=[pltpu.VMEM((1024, 1024), F32)],
        compiler_params=params(60),
        cost_estimate=cost(7),
        name="first_part",
    )(table, back, rows, tw, *after)


def join_kernel(keep_ref, got_ref, second_ref, after_ref, out_ref):
    for m in range(16):
        out_ref[m, 0] = (keep_ref[m] + got_ref[m].astype(F32)).astype(BF16)
        out_ref[m, 1] = second_ref[m]


def join(keep, got, second, after):
    vmem = pl.BlockSpec(memory_space=pltpu.VMEM)
    return pl.pallas_call(
        join_kernel,
        in_specs=[vmem] * 3 + [pl.BlockSpec(memory_space=pl.ANY)],
        out_specs=vmem,
        out_shape=jax.ShapeDtypeStruct((16, 2, 8, 8, 512), BF16),
        compiler_params=params(60),
        cost_estimate=cost(3),
        name="join",
    )(keep, got, second, after)


def plane_sum_kernel(parts_ref, small_ref, after_ref, out_ref):
    small = small_ref[...].astype(BF16)
    for z in range(8):
        for grad in range(2):
            total = parts_ref[0, grad, z].astype(F32)
            for m in range(1, 16):
                total += parts_ref[m, grad, z].astype(F32)
            out_ref[z, grad] = total.astype(BF16)
        for i in range(4):
            out_ref[z, 2 + i] = small[i * 8 : (i + 1) * 8]


def plane_sum(parts, small, after):
    vmem = pl.BlockSpec(memory_space=pltpu.VMEM)
    return pl.pallas_call(
        plane_sum_kernel,
        in_specs=[vmem, vmem, pl.BlockSpec(memory_space=pl.ANY)],
        out_specs=vmem,
        out_shape=jax.ShapeDtypeStruct((8, 6, 8, 512), BF16),
        compiler_params=params(60),
        cost_estimate=cost(2),
        name="plane_sum",
    )(parts, small, after)


def input_kernel(shifted_ref, first_ref, gate_ref, out_ref):
    spread = tn(shifted_ref[...], first_ref[...])
    for q in range(4):
        at = slice(q * 1024, (q + 1) * 1024)
        out_ref[:, at] = (spread[q * 64 : (q + 1) * 64] * gate_ref[:, at].astype(F32)).astype(BF16)


def input_part(shifted, first, gate_in):
    cols = pl.BlockSpec((64, 4096), lambda i: (0, i))
    return pl.pallas_call(
        input_kernel,
        grid=(4,),
        in_specs=[pl.BlockSpec((1024, 256), lambda i: (0, i)), full((1024, 1024)), cols],
        out_specs=cols,
        out_shape=jax.ShapeDtypeStruct(gate_in.shape, BF16),
        compiler_params=params(60),
        cost_estimate=cost(7),
        name="input_part",
    )(shifted, first, gate_in)


def output_kernel(mixer_ref, p0, p1, p2, p3, cot_ref, wd_ref, out_ref, down_ref):
    @pl.when(pl.program_id(0) == 0)
    def _():
        down_ref[...] = jnp.zeros_like(down_ref)

    permuted = jnp.concatenate([p[...] for p in (p0, p1, p2, p3)], axis=0)
    out_ref[...] = (mixer_ref[...].astype(F32) + tn(wd_ref[...], permuted)).astype(BF16)
    down_ref[...] += nt(permuted, cot_ref[...])


def output_part(mixer, parts, cotangent, wd):
    cols = pl.BlockSpec((64, 4096), lambda i: (0, i))
    part = pl.BlockSpec((32, 4096), lambda i: (0, i))
    return pl.pallas_call(
        output_kernel,
        grid=(4,),
        in_specs=[cols] + [part] * 4 + [cols, full(wd.shape)],
        out_specs=[cols, full((128, 64))],
        out_shape=[jax.ShapeDtypeStruct(mixer.shape, BF16), jax.ShapeDtypeStruct((128, 64), F32)],
        compiler_params=params(60),
        cost_estimate=cost(8),
        name="output_part",
    )(mixer, *parts, cotangent, wd)


def swap(values, axis, bit):
    size = int(np.prod([SIZES[AXES.index(a)] for a in ((axis,) if isinstance(axis, str) else axis)]))
    return lax.ppermute(values, axis, [(i, i ^ bit) for i in range(size)])


def chan_swap(parts):
    return [parts[0]] + [swap(parts[i], CHAN, i) for i in (1, 2, 3)]


def start_gather(first, second, core, after):
    both = jnp.stack([first, second]).reshape(2, 4, 2, 512)
    mine = lax.dynamic_index_in_dim(both, core, 2, keepdims=False)
    theirs = lax.dynamic_index_in_dim(both, 1 - core, 2, keepdims=False)
    theirs = swap(theirs, "core", 1)
    rows = jnp.where(
        core == 0,
        jnp.concatenate([mine, theirs], axis=1),
        jnp.concatenate([theirs, mine], axis=1),
    )
    column = lax.all_to_all(fan(rows, 8, after), "z", 0, 0, tiled=True)
    return column


def local(tokens, gate_in, gate_out, twiddle, first_factor, second_factor, w_up, w_down, cotangent):
    core = lax.axis_index("core")
    chan = lax.axis_index(CHAN)
    order = chan ^ jnp.arange(4, dtype=jnp.int32)
    table = jnp.concatenate([jnp.arange(16, dtype=jnp.int32), core.astype(jnp.int32).reshape(1)])
    wd = w_down[0].reshape(4, 32, 64)[order].reshape(128, 64)
    wu = w_up[0].reshape(64, 4, 32)[:, order].reshape(64, 128)

    second_turned = jnp.swapaxes(second_factor.reshape(4, 64, 16), 1, 2).reshape(4, 1024)
    grads = grads_part(cotangent, wd)
    column = start_gather(first_factor, second_turned, core, [grads[0]])
    rows = gated_part(tokens, gate_in)
    grads = chan_swap(grads)
    plane = lax.all_to_all(fan(column, 16, [grads[1], grads[2], rows]), PLANE, 0, 0, tiled=True)
    first_half, second_half = plane[:, :, 0], plane[:, :, 1]
    first = assemble(first_half, swap(first_half, "core", 1), table)
    seg = segment(first, rows, twiddle)
    moved = lax.all_to_all(seg.reshape(64, 16, 1024), SEQ, 0, 0, tiled=True).reshape(1024, 1024)
    second = assemble(second_half, swap(second_half, "core", 1), table)
    back, left, weighted, mixer, *rest = middle(moved, second, gate_out, cotangent, grads, wu)
    acts, up = rest[:4], rest[4]
    returned = lax.all_to_all(back.reshape(64, 16, 1024), SEQ, 0, 0, tiled=True).reshape(1024, 1024)
    acts = chan_swap(acts)
    second_send, second_keep = second_part(table, weighted, left)
    second_total = (second_keep + swap(second_send, "core", 1).astype(F32)).astype(BF16)
    mixed_out, down = output_part(mixer, acts, cotangent, wd)
    up = up.reshape(64, 4, 32)[:, order].reshape(64, 128)
    down = down.reshape(4, 32, 64)[order].reshape(128, 64)
    small = jnp.concatenate([up.reshape(16, 512), down.reshape(16, 512)], axis=0)
    first_send, first_keep, shifted = first_part(
        table, returned, rows, twiddle, [mixed_out, second_total]
    )
    small = (small + swap(small, "x", 1)) + (swap(small, "x", 2) + swap(small, "x", 3))
    joined = join(first_keep, swap(first_send, "core", 1), second_total, small)
    parts = lax.all_to_all(joined, PLANE, 0, 0, tiled=True)
    input_grad = input_part(shifted, first, gate_in)
    small = small + swap(small, "yh", 1)
    both = lax.all_to_all(plane_sum(parts, small, input_grad), "z", 0, 0, tiled=True)
    both = jnp.sum(both.astype(F32), axis=0)
    small = both[2:].reshape(32, 512)
    both = both[:2].reshape(2, 2, 4, 512)
    mine = lax.dynamic_index_in_dim(both, core, 1, keepdims=False)
    theirs = swap(lax.dynamic_index_in_dim(both, 1 - core, 1, keepdims=False), "core", 1)
    both = jnp.where(
        core == 0,
        jnp.concatenate([mine, theirs], axis=2),
        jnp.concatenate([theirs, mine], axis=2),
    )
    return (
        mixed_out,
        input_grad,
        both[0],
        jnp.swapaxes(both[1].reshape(4, 16, 64), 1, 2).reshape(4, 1024),
        small[:16].reshape(1, 64, 128),
        small[16:].reshape(1, 128, 64),
    )


def solution(mesh):
    fine = Mesh(mesh.devices.reshape(SIZES), AXES)
    wide = P(CHAN, SEQ)
    factor = P(AXES, None)
    weight = P(CHAN, None, None)
    return jax.shard_map(
        local,
        mesh=fine,
        in_specs=(wide, wide, wide, P(SEQ, None), factor, factor, weight, weight, wide),
        out_specs=(wide, wide, factor, factor, weight, weight),
        check_vma=False,
    )
```

```python
import functools

import jax
import jax.numpy as jnp
import numpy as np
from jax import lax
from jax.experimental import pallas as pl
from jax.experimental.pallas import tpu as pltpu
from jax.sharding import Mesh
from jax.sharding import PartitionSpec as P

AXES = ("z", "yh", "x", "yl", "core")
SIZES = (8, 2, 4, 2, 2)
SEQ = ("z", "yh", "x")
CHAN = ("yl", "core")
PLANE = ("yh", "x", "yl")
F32 = jnp.float32
BF16 = jnp.bfloat16
MIB = 1024 * 1024


def params(mib, **kw):
    return pltpu.CompilerParams(vmem_limit_bytes=mib * MIB, **kw)


def cost(us, flops=0):
    return pl.CostEstimate(flops=flops, bytes_accessed=int(us * 3.0e3), transcendentals=0)


def full(shape):
    return pl.BlockSpec(shape, lambda i: (0,) * len(shape))


def nt(a, b):
    return lax.dot_general(a, b, (((1,), (1,)), ((), ())), preferred_element_type=F32)


def nn(a, b):
    return lax.dot_general(a, b, (((1,), (0,)), ((), ())), preferred_element_type=F32)


def tn(a, b):
    return lax.dot_general(a, b, (((0,), (0,)), ((), ())), preferred_element_type=F32)


def grads_kernel(cot_ref, wd_ref, *grad_refs):
    grad = nn(wd_ref[...], cot_ref[...]).astype(BF16)
    for i, ref in enumerate(grad_refs):
        ref[...] = grad[i * 32 : (i + 1) * 32]


def grads_part(cotangent, wd):
    chan, positions = cotangent.shape
    part = pl.BlockSpec((32, 4096), lambda i: (0, i))
    return pl.pallas_call(
        grads_kernel,
        grid=(positions // 4096,),
        in_specs=[pl.BlockSpec((chan, 4096), lambda i: (0, i)), full(wd.shape)],
        out_specs=[part] * 4,
        out_shape=[jax.ShapeDtypeStruct((32, positions), BF16)] * 4,
        compiler_params=params(60),
        cost_estimate=cost(4),
        name="grads_part",
    )(cotangent, wd)


def gated_kernel(tok_ref, gate_ref, rows_ref):
    for q in range(4):
        at = slice(q * 1024, (q + 1) * 1024)
        rows_ref[q * 64 : (q + 1) * 64] = (
            tok_ref[:, at].astype(F32) * gate_ref[:, at].astype(F32)
        ).astype(BF16)


def gated_part(tokens, gate_in):
    cols = pl.BlockSpec((64, 4096), lambda i: (0, i))
    return pl.pallas_call(
        gated_kernel,
        grid=(4,),
        in_specs=[cols, cols],
        out_specs=pl.BlockSpec((256, 1024), lambda i: (i, 0)),
        out_shape=jax.ShapeDtypeStruct((1024, 1024), BF16),
        compiler_params=params(60),
        cost_estimate=cost(4),
        name="gated_part",
    )(tokens, gate_in)


def assemble_kernel(factor, table_ref, own_ref, other_ref, out_ref):
    first = table_ref[16] == 0
    for m in range(16):
        at = table_ref[m]
        own, other = own_ref[at, factor], other_ref[at]
        out_ref[:, m, :, :512] = jnp.where(first, own, other)
        out_ref[:, m, :, 512:] = jnp.where(first, other, own)


def assemble(own, other, table, factor):
    out = pl.pallas_call(
        functools.partial(assemble_kernel, factor),
        in_specs=[pl.BlockSpec(memory_space=pltpu.SMEM)] + [pl.BlockSpec(memory_space=pltpu.VMEM)] * 2,
        out_specs=pl.BlockSpec(memory_space=pltpu.VMEM),
        out_shape=jax.ShapeDtypeStruct((8, 16, 8, 1024), BF16),
        compiler_params=params(12),
        cost_estimate=cost(3),
        name="assemble",
    )(table, own, other)
    return out.reshape(1024, 1024)


def fan_kernel(column_ref, *refs):
    for m in range(refs[-1].shape[0]):
        refs[-1][m] = column_ref[...]


def fan_plane_kernel(column_ref, *refs):
    for m in range(16):
        for z in range(8):
            for factor in range(2):
                refs[-1][m, factor, z] = column_ref[z, factor]


def fan(kernel, column, shape, after):
    vmem = pl.BlockSpec(memory_space=pltpu.VMEM)
    return pl.pallas_call(
        kernel,
        in_specs=[vmem] + [pl.BlockSpec(memory_space=pl.ANY)] * len(after),
        out_specs=vmem,
        out_shape=jax.ShapeDtypeStruct(shape, BF16),
        compiler_params=params(10),
        cost_estimate=cost(1),
        name="fan",
    )(column, *after)


def spread_twiddle(tw):
    high = tw.astype(BF16)
    rest = tw - high.astype(F32)
    mid = rest.astype(BF16)
    low = (rest - mid.astype(F32)).astype(BF16)
    terms = jnp.concatenate([high, mid, low], axis=0)
    row = lax.broadcasted_iota(jnp.int32, (48, 1024), 0)
    lane = lax.broadcasted_iota(jnp.int32, (48, 1024), 1)
    pick = jnp.where(row % 16 == lane // 64, 1.0, 0.0).astype(BF16)
    return tn(terms, pick)


def segment_kernel(first_ref, rows_ref, tw_ref, out_ref):
    scale = spread_twiddle(tw_ref[...])
    out_ref[...] = (nt(first_ref[...], rows_ref[...]) * scale).astype(BF16)


def segment(first, rows, tw):
    return pl.pallas_call(
        segment_kernel,
        grid=(4,),
        in_specs=[
            pl.BlockSpec((256, 1024), lambda i: (i, 0)),
            full((1024, 1024)),
            pl.BlockSpec((16, 256), lambda i: (0, i)),
        ],
        out_specs=pl.BlockSpec((256, 1024), lambda i: (i, 0)),
        out_shape=jax.ShapeDtypeStruct((1024, 1024), BF16),
        compiler_params=params(24),
        cost_estimate=cost(6),
        name="segment",
    )(first, rows, tw)


def swap_lanes(values):
    return pltpu.roll(values, 64, 1)


def middle_kernel(
    moved_ref, second_ref, gate_ref, cot_ref, g0, g1, g2, g3, wu_ref,
    back_ref, left_ref, weighted_ref, mixer_ref, a0, a1, a2, a3, up_ref,
    wide_ref, prod_ref,
):
    step = pl.program_id(0)
    grads, acts = (g0, g1, g2, g3), (a0, a1, a2, a3)

    @pl.when(step == 0)
    def _():
        for p in range(8):
            wide_ref[p * 1024 : (p + 1) * 1024] = moved_ref[:, p * 128 : (p + 1) * 128].astype(F32)
        up_ref[...] = jnp.zeros_like(up_ref)

    low = lax.broadcasted_iota(jnp.int32, (64, 128), 1) < 64
    for pair in range(2):
        k = step * 4 + pair * 2
        for p in range(8):
            lanes = slice(p * 128, (p + 1) * 128)
            one = wide_ref[pl.ds(p * 1024 + k, 64, stride=16)]
            two = wide_ref[pl.ds(p * 1024 + k + 1, 64, stride=16)]
            both = jnp.concatenate(
                [jnp.where(low, one, swap_lanes(two)), jnp.where(low, swap_lanes(one), two)], axis=0
            )
            left_ref[pair * 128 : (pair + 1) * 128, lanes] = both.T.astype(BF16)
    prod_ref[...] = nt(left_ref[...], second_ref[...])
    wu = wu_ref[...]
    up = jnp.zeros((64, 128), F32)
    for unit in range(0, 4, 4):
        at = slice(unit * 1024, (unit + 4) * 1024)
        for kk in range(unit, unit + 4):
            cols = slice(kk * 1024, (kk + 1) * 1024)
            gate = gate_ref[:, cols].astype(F32)
            mixer_ref[:, cols] = (prod_ref[kk * 64 : (kk + 1) * 64] * gate).astype(BF16)
        mix = mixer_ref[:, at]
        hidden = tn(wu, mix)
        cum = 0.5 * (1.0 + lax.erf(hidden * 0.7071067811865476))
        act = (hidden * cum).astype(BF16)
        slope = cum + hidden * (jnp.exp(-0.5 * hidden * hidden) * 0.3989422804014327)
        for i in range(4):
            acts[i][:, at] = act[i * 32 : (i + 1) * 32]
        grad = jnp.concatenate([g[:, at] for g in grads], axis=0)
        hgrad = (grad.astype(F32) * slope).astype(BF16)
        up += nt(mix, hgrad)
        mgrad = nn(wu, hgrad)
        for kk in range(unit, unit + 4):
            cols = slice(kk * 1024, (kk + 1) * 1024)
            total = cot_ref[:, cols].astype(F32) + mgrad[:, (kk - unit) * 1024 : (kk - unit + 1) * 1024]
            weighted_ref[kk * 64 : (kk + 1) * 64] = (total * gate_ref[:, cols].astype(F32)).astype(BF16)
    up_ref[...] += up
    prod_ref[...] = nn(weighted_ref[...], second_ref[...])
    for pair in range(2):
        k = step * 4 + pair * 2
        for p in range(8):
            lanes = slice(p * 128, (p + 1) * 128)
            both = prod_ref[pair * 128 : (pair + 1) * 128, lanes].T
            top, bottom = both[:64], both[64:]
            wide_ref[pl.ds(p * 1024 + k, 64, stride=16)] = jnp.where(low, top, swap_lanes(bottom))
            wide_ref[pl.ds(p * 1024 + k + 1, 64, stride=16)] = jnp.where(low, swap_lanes(top), bottom)

    @pl.when(step == 3)
    def _():
        for p in range(8):
            back_ref[:, p * 128 : (p + 1) * 128] = wide_ref[p * 1024 : (p + 1) * 1024].astype(BF16)


def middle(moved, second, gate_out, cotangent, grads, wu):
    chan, positions = gate_out.shape
    cols = pl.BlockSpec((chan, 4096), lambda i: (0, i))
    part = pl.BlockSpec((32, 4096), lambda i: (0, i))
    square = full((1024, 1024))
    rows = pl.BlockSpec((256, 1024), lambda i: (i, 0))
    big = jax.ShapeDtypeStruct((1024, 1024), BF16)
    small = jax.ShapeDtypeStruct((32, positions), BF16)
    return pl.pallas_call(
        middle_kernel,
        grid=(4,),
        in_specs=[square, square, cols, cols] + [part] * 4 + [full(wu.shape)],
        out_specs=[square, rows, rows, cols] + [part] * 4 + [full((64, 128))],
        out_shape=[big, big, big, jax.ShapeDtypeStruct((chan, positions), BF16)]
        + [small] * 4
        + [jax.ShapeDtypeStruct((64, 128), F32)],
        scratch_shapes=[pltpu.VMEM((8192, 128), F32), pltpu.VMEM((256, 1024), F32)],
        compiler_params=params(44),
        cost_estimate=cost(25),
        name="middle",
    )(moved, second, gate_out, cotangent, *grads, wu)


def split_columns(table_ref, total, send_ref, keep_ref):
    first = table_ref[16] == 0
    for m in range(16):
        at = table_ref[m]
        for z in range(8):
            row = z * 128 + m * 8
            lo, hi = total[row : row + 8, :512], total[row : row + 8, 512:]
            send_ref[at, z] = jnp.where(first, hi, lo).astype(BF16)
            keep_ref[at, z] = jnp.where(first, lo, hi)


def second_kernel(table_ref, weighted_ref, left_ref, send_ref, keep_ref, total_ref):
    total_ref[...] = tn(weighted_ref[...], left_ref[...])
    split_columns(table_ref, total_ref, send_ref, keep_ref)


HALF = [
    jax.ShapeDtypeStruct((16, 8, 8, 512), BF16),
    jax.ShapeDtypeStruct((16, 8, 8, 512), F32),
]


def second_part(table, weighted, left):
    vmem = pl.BlockSpec(memory_space=pltpu.VMEM)
    return pl.pallas_call(
        second_kernel,
        in_specs=[pl.BlockSpec(memory_space=pltpu.SMEM), vmem, vmem],
        out_specs=[vmem, vmem],
        out_shape=HALF,
        scratch_shapes=[pltpu.VMEM((1024, 1024), F32)],
        compiler_params=params(28),
        cost_estimate=cost(7),
        name="second_part",
    )(table, weighted, left)


def first_kernel(table_ref, back_ref, rows_ref, tw_ref, *refs):
    send_ref, keep_ref, shifted_ref, total_ref = refs[-4:]
    for i in range(4):
        at = slice(i * 256, (i + 1) * 256)
        scale = spread_twiddle(tw_ref[:, at])
        shifted_ref[at] = (back_ref[at].astype(F32) * scale).astype(BF16)
    total_ref[...] = nn(shifted_ref[...], rows_ref[...])
    split_columns(table_ref, total_ref, send_ref, keep_ref)


def first_part(table, back, rows, tw, after):
    vmem = pl.BlockSpec(memory_space=pltpu.VMEM)
    return pl.pallas_call(
        first_kernel,
        in_specs=[pl.BlockSpec(memory_space=pltpu.SMEM), vmem, vmem, vmem]
        + [pl.BlockSpec(memory_space=pl.ANY)] * len(after),
        out_specs=[vmem, vmem, vmem],
        out_shape=HALF + [jax.ShapeDtypeStruct((1024, 1024), BF16)],
        scratch_shapes=[pltpu.VMEM((1024, 1024), F32)],
        compiler_params=params(28),
        cost_estimate=cost(7),
        name="first_part",
    )(table, back, rows, tw, *after)


def join_kernel(keep_ref, got_ref, second_keep_ref, second_got_ref, out_ref):
    for m in range(16):
        out_ref[m, 0] = (keep_ref[m] + got_ref[m].astype(F32)).astype(BF16)
        out_ref[m, 1] = (second_keep_ref[m] + second_got_ref[m].astype(F32)).astype(BF16)


def join(keep, got, second_keep, second_got):
    vmem = pl.BlockSpec(memory_space=pltpu.VMEM)
    return pl.pallas_call(
        join_kernel,
        in_specs=[vmem] * 4,
        out_specs=vmem,
        out_shape=jax.ShapeDtypeStruct((16, 2, 8, 8, 512), BF16),
        compiler_params=params(20),
        cost_estimate=cost(3),
        name="join",
    )(keep, got, second_keep, second_got)


def plane_sum_kernel(parts_ref, small_ref, out_ref):
    small = small_ref[...].astype(BF16)
    for z in range(8):
        for grad in range(2):
            total = parts_ref[0, grad, z].astype(F32)
            for m in range(1, 16):
                total += parts_ref[m, grad, z].astype(F32)
            out_ref[z, grad] = total.astype(BF16)
        for i in range(4):
            out_ref[z, 2 + i] = small[i * 8 : (i + 1) * 8]


def plane_sum(parts, small):
    vmem = pl.BlockSpec(memory_space=pltpu.VMEM)
    return pl.pallas_call(
        plane_sum_kernel,
        in_specs=[vmem, vmem],
        out_specs=vmem,
        out_shape=jax.ShapeDtypeStruct((8, 6, 8, 512), BF16),
        compiler_params=params(12),
        cost_estimate=cost(2),
        name="plane_sum",
    )(parts, small)


def z_sum_kernel(parts_ref, after_ref, out_ref):
    total = parts_ref[0].astype(F32)
    for z in range(1, 8):
        total += parts_ref[z].astype(F32)
    out_ref[...] = total


def z_sum(parts, after):
    vmem = pl.BlockSpec(memory_space=pltpu.VMEM)
    return pl.pallas_call(
        z_sum_kernel,
        in_specs=[vmem, pl.BlockSpec(memory_space=pl.ANY)],
        out_specs=vmem,
        out_shape=jax.ShapeDtypeStruct(parts.shape[1:], F32),
        compiler_params=params(10),
        cost_estimate=cost(1),
        name="z_sum",
    )(parts, after)


def input_kernel(shifted_ref, first_ref, gate_ref, after_ref, out_ref):
    spread = tn(shifted_ref[...], first_ref[...])
    for q in range(4):
        at = slice(q * 1024, (q + 1) * 1024)
        out_ref[:, at] = (spread[q * 64 : (q + 1) * 64] * gate_ref[:, at].astype(F32)).astype(BF16)


def input_part(shifted, first, gate_in, after):
    cols = pl.BlockSpec((64, 4096), lambda i: (0, i))
    return pl.pallas_call(
        input_kernel,
        grid=(4,),
        in_specs=[
            pl.BlockSpec((1024, 256), lambda i: (0, i)),
            full((1024, 1024)),
            cols,
            pl.BlockSpec(memory_space=pl.ANY),
        ],
        out_specs=cols,
        out_shape=jax.ShapeDtypeStruct(gate_in.shape, BF16),
        compiler_params=params(60),
        cost_estimate=cost(7),
        name="input_part",
    )(shifted, first, gate_in, after)


def output_kernel(mixer_ref, p0, p1, p2, p3, cot_ref, wd_ref, out_ref, down_ref):
    @pl.when(pl.program_id(0) == 0)
    def _():
        down_ref[...] = jnp.zeros_like(down_ref)

    permuted = jnp.concatenate([p[...] for p in (p0, p1, p2, p3)], axis=0)
    out_ref[...] = (mixer_ref[...].astype(F32) + tn(wd_ref[...], permuted)).astype(BF16)
    down_ref[...] += nt(permuted, cot_ref[...])


def output_part(mixer, parts, cotangent, wd):
    cols = pl.BlockSpec((64, 4096), lambda i: (0, i))
    part = pl.BlockSpec((32, 4096), lambda i: (0, i))
    return pl.pallas_call(
        output_kernel,
        grid=(4,),
        in_specs=[cols] + [part] * 4 + [cols, full(wd.shape)],
        out_specs=[cols, full((128, 64))],
        out_shape=[jax.ShapeDtypeStruct(mixer.shape, BF16), jax.ShapeDtypeStruct((128, 64), F32)],
        compiler_params=params(60),
        cost_estimate=cost(8),
        name="output_part",
    )(mixer, *parts, cotangent, wd)


def swap(values, axis, bit):
    size = int(np.prod([SIZES[AXES.index(a)] for a in ((axis,) if isinstance(axis, str) else axis)]))
    return lax.ppermute(values, axis, [(i, i ^ bit) for i in range(size)])


def chan_swap(parts):
    return [parts[0]] + [swap(parts[i], CHAN, i) for i in (1, 2, 3)]


def start_gather(first, second, core, after):
    both = jnp.stack([first, second]).reshape(2, 4, 2, 512)
    mine = lax.dynamic_index_in_dim(both, core, 2, keepdims=False)
    theirs = lax.dynamic_index_in_dim(both, 1 - core, 2, keepdims=False)
    theirs = swap(theirs, "core", 1)
    rows = jnp.where(
        core == 0,
        jnp.concatenate([mine, theirs], axis=1),
        jnp.concatenate([theirs, mine], axis=1),
    )
    column = lax.all_to_all(fan(fan_kernel, rows, (8,) + rows.shape, after), "z", 0, 0, tiled=True)
    return column


def local(tokens, gate_in, gate_out, twiddle, first_factor, second_factor, w_up, w_down, cotangent):
    core = lax.axis_index("core")
    chan = lax.axis_index(CHAN)
    order = chan ^ jnp.arange(4, dtype=jnp.int32)
    table = jnp.concatenate([jnp.arange(16, dtype=jnp.int32), core.astype(jnp.int32).reshape(1)])
    wd = w_down[0].reshape(4, 32, 64)[order].reshape(128, 64)
    wu = w_up[0].reshape(64, 4, 32)[:, order].reshape(64, 128)

    second_turned = jnp.swapaxes(second_factor.reshape(4, 64, 16), 1, 2).reshape(4, 1024)
    grads = grads_part(cotangent, wd)
    column = start_gather(first_factor, second_turned, core, [grads[0]])
    rows = gated_part(tokens, gate_in)
    grads = chan_swap(grads)
    plane = lax.all_to_all(
        fan(fan_plane_kernel, column, (16, 2, 8, 8, 512), [grads[1], grads[2], rows]), PLANE, 0, 0, tiled=True
    )
    first = assemble(plane, swap(plane[:, 0], "core", 1), table, 0)
    seg = segment(first, rows, twiddle)
    moved = lax.all_to_all(seg.reshape(64, 16, 1024), SEQ, 0, 0, tiled=True).reshape(1024, 1024)
    second = assemble(plane, swap(plane[:, 1], "core", 1), table, 1)
    back, left, weighted, mixer, *rest = middle(moved, second, gate_out, cotangent, grads, wu)
    acts, up = rest[:4], rest[4]
    returned = lax.all_to_all(back.reshape(64, 16, 1024), SEQ, 0, 0, tiled=True).reshape(1024, 1024)
    acts = chan_swap(acts)
    second_send, second_keep = second_part(table, weighted, left)
    second_got = swap(second_send, "core", 1)
    mixed_out, down = output_part(mixer, acts, cotangent, wd)
    up = up.reshape(64, 4, 32)[:, order].reshape(64, 128)
    down = down.reshape(4, 32, 64)[order].reshape(128, 64)
    small = jnp.concatenate([up.reshape(16, 512), down.reshape(16, 512)], axis=0)
    first_send, first_keep, shifted = first_part(
        table, returned, rows, twiddle, [mixed_out, second_got]
    )
    small = (small + swap(small, "x", 1)) + (swap(small, "x", 2) + swap(small, "x", 3))
    joined = join(first_keep, swap(first_send, "core", 1), second_keep, second_got)
    parts = lax.all_to_all(joined, PLANE, 0, 0, tiled=True)
    small = small + swap(small, "yh", 1)
    both = plane_sum(parts, small)
    input_grad = input_part(shifted, first, gate_in, both)
    both = lax.all_to_all(both, "z", 0, 0, tiled=True)
    both = z_sum(both, input_grad)
    small = both[2:].reshape(32, 512)
    both = both[:2].reshape(2, 2, 4, 512)
    mine = lax.dynamic_index_in_dim(both, core, 1, keepdims=False)
    theirs = swap(lax.dynamic_index_in_dim(both, 1 - core, 1, keepdims=False), "core", 1)
    both = jnp.where(
        core == 0,
        jnp.concatenate([mine, theirs], axis=2),
        jnp.concatenate([theirs, mine], axis=2),
    )
    return (
        mixed_out,
        input_grad,
        both[0],
        jnp.swapaxes(both[1].reshape(4, 16, 64), 1, 2).reshape(4, 1024),
        small[:16].reshape(1, 64, 128),
        small[16:].reshape(1, 128, 64),
    )


def solution(mesh):
    fine = Mesh(mesh.devices.reshape(SIZES), AXES)
    wide = P(CHAN, SEQ)
    factor = P(AXES, None)
    weight = P(CHAN, None, None)
    return jax.shard_map(
        local,
        mesh=fine,
        in_specs=(wide, wide, wide, P(SEQ, None), factor, factor, weight, weight, wide),
        out_specs=(wide, wide, factor, factor, weight, weight),
        check_vma=False,
    )
```

```python
import functools

import jax
import jax.numpy as jnp
import numpy as np
from jax import lax
from jax.experimental import pallas as pl
from jax.experimental.pallas import tpu as pltpu
from jax.sharding import Mesh
from jax.sharding import PartitionSpec as P

AXES = ("z", "yh", "x", "yl", "core")
SIZES = (8, 2, 4, 2, 2)
SEQ = ("z", "yh", "x")
CHAN = ("yl", "core")
PLANE = ("yh", "x", "yl")
F32 = jnp.float32
BF16 = jnp.bfloat16
MIB = 1024 * 1024


def params(mib, **kw):
    return pltpu.CompilerParams(vmem_limit_bytes=mib * MIB, **kw)


def cost(us, flops=0):
    return pl.CostEstimate(flops=flops, bytes_accessed=int(us * 3.0e3), transcendentals=0)


def full(shape):
    return pl.BlockSpec(shape, lambda i: (0,) * len(shape))


def nt(a, b):
    return lax.dot_general(a, b, (((1,), (1,)), ((), ())), preferred_element_type=F32)


def nn(a, b):
    return lax.dot_general(a, b, (((1,), (0,)), ((), ())), preferred_element_type=F32)


def tn(a, b):
    return lax.dot_general(a, b, (((0,), (0,)), ((), ())), preferred_element_type=F32)


def grads_kernel(cot_ref, wd_ref, *grad_refs):
    grad = nn(wd_ref[...], cot_ref[...]).astype(BF16)
    for i, ref in enumerate(grad_refs):
        ref[...] = grad[i * 32 : (i + 1) * 32]


def grads_part(cotangent, wd):
    chan, positions = cotangent.shape
    part = pl.BlockSpec((32, 4096), lambda i: (0, i))
    return pl.pallas_call(
        grads_kernel,
        grid=(positions // 4096,),
        in_specs=[pl.BlockSpec((chan, 4096), lambda i: (0, i)), full(wd.shape)],
        out_specs=[part] * 4,
        out_shape=[jax.ShapeDtypeStruct((32, positions), BF16)] * 4,
        compiler_params=params(60),
        cost_estimate=cost(4),
        name="grads_part",
    )(cotangent, wd)


def gated_kernel(tok_ref, gate_ref, rows_ref):
    for q in range(4):
        at = slice(q * 1024, (q + 1) * 1024)
        rows_ref[q * 64 : (q + 1) * 64] = (
            tok_ref[:, at].astype(F32) * gate_ref[:, at].astype(F32)
        ).astype(BF16)


def gated_part(tokens, gate_in):
    cols = pl.BlockSpec((64, 4096), lambda i: (0, i))
    return pl.pallas_call(
        gated_kernel,
        grid=(4,),
        in_specs=[cols, cols],
        out_specs=pl.BlockSpec((256, 1024), lambda i: (i, 0)),
        out_shape=pltpu.HBM((1024, 1024), BF16),
        compiler_params=params(60),
        cost_estimate=cost(4),
        name="gated_part",
    )(tokens, gate_in)


def assemble_kernel(factor, table_ref, own_ref, other_ref, out_ref):
    first = table_ref[16] == 0
    for m in range(16):
        at = table_ref[m]
        own, other = own_ref[at, factor], other_ref[at]
        out_ref[:, m, :, :512] = jnp.where(first, own, other)
        out_ref[:, m, :, 512:] = jnp.where(first, other, own)


def assemble(own, other, table, factor):
    out = pl.pallas_call(
        functools.partial(assemble_kernel, factor),
        in_specs=[pl.BlockSpec(memory_space=pltpu.SMEM)] + [pl.BlockSpec(memory_space=pltpu.VMEM)] * 2,
        out_specs=pl.BlockSpec(memory_space=pltpu.VMEM),
        out_shape=jax.ShapeDtypeStruct((8, 16, 8, 1024), BF16),
        compiler_params=params(12),
        cost_estimate=cost(3),
        name="assemble",
    )(table, own, other)
    return out.reshape(1024, 1024)


def fan_kernel(column_ref, *refs):
    for m in range(refs[-1].shape[0]):
        refs[-1][m] = column_ref[...]


def fan_plane_kernel(column_ref, *refs):
    for m in range(16):
        for z in range(8):
            for factor in range(2):
                refs[-1][m, factor, z] = column_ref[z, factor]


def fan(kernel, column, shape, after):
    vmem = pl.BlockSpec(memory_space=pltpu.VMEM)
    return pl.pallas_call(
        kernel,
        in_specs=[vmem] + [pl.BlockSpec(memory_space=pl.ANY)] * len(after),
        out_specs=vmem,
        out_shape=pltpu.HBM(shape, BF16),
        compiler_params=params(10),
        cost_estimate=cost(1),
        name="fan",
    )(column, *after)


def spread_twiddle(tw):
    high = tw.astype(BF16)
    rest = tw - high.astype(F32)
    mid = rest.astype(BF16)
    low = (rest - mid.astype(F32)).astype(BF16)
    terms = jnp.concatenate([high, mid, low], axis=0)
    row = lax.broadcasted_iota(jnp.int32, (48, 1024), 0)
    lane = lax.broadcasted_iota(jnp.int32, (48, 1024), 1)
    pick = jnp.where(row % 16 == lane // 64, 1.0, 0.0).astype(BF16)
    return tn(terms, pick)


def segment_kernel(first_ref, rows_ref, tw_ref, out_ref):
    scale = spread_twiddle(tw_ref[...])
    out_ref[...] = (nt(first_ref[...], rows_ref[...]) * scale).astype(BF16)


def segment(first, rows, tw):
    return pl.pallas_call(
        segment_kernel,
        grid=(4,),
        in_specs=[
            pl.BlockSpec((256, 1024), lambda i: (i, 0)),
            full((1024, 1024)),
            pl.BlockSpec((16, 256), lambda i: (0, i)),
        ],
        out_specs=pl.BlockSpec((256, 1024), lambda i: (i, 0)),
        out_shape=pltpu.HBM((1024, 1024), BF16),
        compiler_params=params(24),
        cost_estimate=cost(6),
        name="segment",
    )(first, rows, tw)


def swap_lanes(values):
    return pltpu.roll(values, 64, 1)


def middle_kernel(
    moved_ref, second_ref, gate_ref, cot_ref, g0, g1, g2, g3, wu_ref,
    back_ref, left_ref, weighted_ref, mixer_ref, a0, a1, a2, a3, up_ref,
    wide_ref, prod_ref,
):
    step = pl.program_id(0)
    grads, acts = (g0, g1, g2, g3), (a0, a1, a2, a3)

    @pl.when(step == 0)
    def _():
        for p in range(8):
            wide_ref[p * 1024 : (p + 1) * 1024] = moved_ref[:, p * 128 : (p + 1) * 128].astype(F32)
        up_ref[...] = jnp.zeros_like(up_ref)

    low = lax.broadcasted_iota(jnp.int32, (64, 128), 1) < 64
    for pair in range(2):
        k = step * 4 + pair * 2
        for p in range(8):
            lanes = slice(p * 128, (p + 1) * 128)
            one = wide_ref[pl.ds(p * 1024 + k, 64, stride=16)]
            two = wide_ref[pl.ds(p * 1024 + k + 1, 64, stride=16)]
            both = jnp.concatenate(
                [jnp.where(low, one, swap_lanes(two)), jnp.where(low, swap_lanes(one), two)], axis=0
            )
            left_ref[pair * 128 : (pair + 1) * 128, lanes] = both.T.astype(BF16)
    prod_ref[...] = nt(left_ref[...], second_ref[...])
    wu = wu_ref[...]
    up = jnp.zeros((64, 128), F32)
    for unit in range(0, 4, 4):
        at = slice(unit * 1024, (unit + 4) * 1024)
        for kk in range(unit, unit + 4):
            cols = slice(kk * 1024, (kk + 1) * 1024)
            gate = gate_ref[:, cols].astype(F32)
            mixer_ref[:, cols] = (prod_ref[kk * 64 : (kk + 1) * 64] * gate).astype(BF16)
        mix = mixer_ref[:, at]
        hidden = tn(wu, mix)
        cum = 0.5 * (1.0 + lax.erf(hidden * 0.7071067811865476))
        act = (hidden * cum).astype(BF16)
        slope = cum + hidden * (jnp.exp(-0.5 * hidden * hidden) * 0.3989422804014327)
        for i in range(4):
            acts[i][:, at] = act[i * 32 : (i + 1) * 32]
        grad = jnp.concatenate([g[:, at] for g in grads], axis=0)
        hgrad = (grad.astype(F32) * slope).astype(BF16)
        up += nt(mix, hgrad)
        mgrad = nn(wu, hgrad)
        for kk in range(unit, unit + 4):
            cols = slice(kk * 1024, (kk + 1) * 1024)
            total = cot_ref[:, cols].astype(F32) + mgrad[:, (kk - unit) * 1024 : (kk - unit + 1) * 1024]
            weighted_ref[kk * 64 : (kk + 1) * 64] = (total * gate_ref[:, cols].astype(F32)).astype(BF16)
    up_ref[...] += up
    prod_ref[...] = nn(weighted_ref[...], second_ref[...])
    for pair in range(2):
        k = step * 4 + pair * 2
        for p in range(8):
            lanes = slice(p * 128, (p + 1) * 128)
            both = prod_ref[pair * 128 : (pair + 1) * 128, lanes].T
            top, bottom = both[:64], both[64:]
            wide_ref[pl.ds(p * 1024 + k, 64, stride=16)] = jnp.where(low, top, swap_lanes(bottom))
            wide_ref[pl.ds(p * 1024 + k + 1, 64, stride=16)] = jnp.where(low, swap_lanes(top), bottom)

    @pl.when(step == 3)
    def _():
        for p in range(8):
            back_ref[:, p * 128 : (p + 1) * 128] = wide_ref[p * 1024 : (p + 1) * 1024].astype(BF16)


def middle(moved, second, gate_out, cotangent, grads, wu):
    chan, positions = gate_out.shape
    cols = pl.BlockSpec((chan, 4096), lambda i: (0, i))
    part = pl.BlockSpec((32, 4096), lambda i: (0, i))
    square = full((1024, 1024))
    rows = pl.BlockSpec((256, 1024), lambda i: (i, 0))
    big = pltpu.HBM((1024, 1024), BF16)
    small = pltpu.HBM((32, positions), BF16)
    return pl.pallas_call(
        middle_kernel,
        grid=(4,),
        in_specs=[square, square, cols, cols] + [part] * 4 + [full(wu.shape)],
        out_specs=[square, rows, rows, cols] + [part] * 4 + [full((64, 128))],
        out_shape=[big, big, big, pltpu.HBM((chan, positions), BF16)]
        + [small] * 4
        + [jax.ShapeDtypeStruct((64, 128), F32)],
        scratch_shapes=[pltpu.VMEM((8192, 128), F32), pltpu.VMEM((256, 1024), F32)],
        compiler_params=params(44),
        cost_estimate=cost(25),
        name="middle",
    )(moved, second, gate_out, cotangent, *grads, wu)


def split_columns(table_ref, total, send_ref, keep_ref):
    first = table_ref[16] == 0
    for m in range(16):
        at = table_ref[m]
        for z in range(8):
            row = z * 128 + m * 8
            lo, hi = total[row : row + 8, :512], total[row : row + 8, 512:]
            send_ref[at, z] = jnp.where(first, hi, lo).astype(BF16)
            keep_ref[at, z] = jnp.where(first, lo, hi)


def second_kernel(table_ref, weighted_ref, left_ref, send_ref, keep_ref, total_ref):
    total_ref[...] = tn(weighted_ref[...], left_ref[...])
    split_columns(table_ref, total_ref, send_ref, keep_ref)


HALF = [
    jax.ShapeDtypeStruct((16, 8, 8, 512), BF16),
    jax.ShapeDtypeStruct((16, 8, 8, 512), F32),
]


def second_part(table, weighted, left):
    vmem = pl.BlockSpec(memory_space=pltpu.VMEM)
    return pl.pallas_call(
        second_kernel,
        in_specs=[pl.BlockSpec(memory_space=pltpu.SMEM), vmem, vmem],
        out_specs=[vmem, vmem],
        out_shape=HALF,
        scratch_shapes=[pltpu.VMEM((1024, 1024), F32)],
        compiler_params=params(28),
        cost_estimate=cost(7),
        name="second_part",
    )(table, weighted, left)


def first_kernel(table_ref, back_ref, rows_ref, tw_ref, *refs):
    send_ref, keep_ref, shifted_ref, total_ref = refs[-4:]
    for i in range(4):
        at = slice(i * 256, (i + 1) * 256)
        scale = spread_twiddle(tw_ref[:, at])
        shifted_ref[at] = (back_ref[at].astype(F32) * scale).astype(BF16)
    total_ref[...] = nn(shifted_ref[...], rows_ref[...])
    split_columns(table_ref, total_ref, send_ref, keep_ref)


def first_part(table, back, rows, tw, after):
    vmem = pl.BlockSpec(memory_space=pltpu.VMEM)
    return pl.pallas_call(
        first_kernel,
        in_specs=[pl.BlockSpec(memory_space=pltpu.SMEM), vmem, vmem, vmem]
        + [pl.BlockSpec(memory_space=pl.ANY)] * len(after),
        out_specs=[vmem, vmem, vmem],
        out_shape=HALF + [pltpu.HBM((1024, 1024), BF16)],
        scratch_shapes=[pltpu.VMEM((1024, 1024), F32)],
        compiler_params=params(28),
        cost_estimate=cost(7),
        name="first_part",
    )(table, back, rows, tw, *after)


def join_kernel(keep_ref, got_ref, second_keep_ref, second_got_ref, out_ref):
    for m in range(16):
        out_ref[m, 0] = (keep_ref[m] + got_ref[m].astype(F32)).astype(BF16)
        out_ref[m, 1] = (second_keep_ref[m] + second_got_ref[m].astype(F32)).astype(BF16)


def join(keep, got, second_keep, second_got):
    vmem = pl.BlockSpec(memory_space=pltpu.VMEM)
    return pl.pallas_call(
        join_kernel,
        in_specs=[vmem] * 4,
        out_specs=vmem,
        out_shape=pltpu.HBM((16, 2, 8, 8, 512), BF16),
        compiler_params=params(20),
        cost_estimate=cost(3),
        name="join",
    )(keep, got, second_keep, second_got)


def plane_sum_kernel(parts_ref, small_ref, out_ref):
    small = small_ref[...].astype(BF16)
    for z in range(8):
        for grad in range(2):
            total = parts_ref[0, grad, z].astype(F32)
            for m in range(1, 16):
                total += parts_ref[m, grad, z].astype(F32)
            out_ref[z, grad] = total.astype(BF16)
        for i in range(4):
            out_ref[z, 2 + i] = small[i * 8 : (i + 1) * 8]


def plane_sum(parts, small):
    vmem = pl.BlockSpec(memory_space=pltpu.VMEM)
    return pl.pallas_call(
        plane_sum_kernel,
        in_specs=[vmem, vmem],
        out_specs=vmem,
        out_shape=jax.ShapeDtypeStruct((8, 6, 8, 512), BF16),
        compiler_params=params(12),
        cost_estimate=cost(2),
        name="plane_sum",
    )(parts, small)


def z_sum_kernel(parts_ref, after_ref, out_ref):
    total = parts_ref[0].astype(F32)
    for z in range(1, 8):
        total += parts_ref[z].astype(F32)
    out_ref[...] = total


def z_sum(parts, after):
    vmem = pl.BlockSpec(memory_space=pltpu.VMEM)
    return pl.pallas_call(
        z_sum_kernel,
        in_specs=[vmem, pl.BlockSpec(memory_space=pl.ANY)],
        out_specs=vmem,
        out_shape=jax.ShapeDtypeStruct(parts.shape[1:], F32),
        compiler_params=params(10),
        cost_estimate=cost(1),
        name="z_sum",
    )(parts, after)


def input_kernel(shifted_ref, first_ref, gate_ref, after_ref, out_ref, done_ref):
    done_ref[...] = jnp.zeros_like(done_ref)
    spread = tn(shifted_ref[...], first_ref[...])
    for q in range(4):
        at = slice(q * 1024, (q + 1) * 1024)
        out_ref[:, at] = (spread[q * 64 : (q + 1) * 64] * gate_ref[:, at].astype(F32)).astype(BF16)


def input_part(shifted, first, gate_in, after):
    cols = pl.BlockSpec((64, 4096), lambda i: (0, i))
    return pl.pallas_call(
        input_kernel,
        grid=(4,),
        in_specs=[
            pl.BlockSpec((1024, 256), lambda i: (0, i)),
            full((1024, 1024)),
            cols,
            pl.BlockSpec(memory_space=pl.ANY),
        ],
        out_specs=[cols, full((8, 128))],
        out_shape=[
            jax.ShapeDtypeStruct(gate_in.shape, BF16),
            jax.ShapeDtypeStruct((8, 128), F32),
        ],
        compiler_params=params(60),
        cost_estimate=cost(7),
        name="input_part",
    )(shifted, first, gate_in, after)


def output_kernel(mixer_ref, p0, p1, p2, p3, cot_ref, wd_ref, out_ref, down_ref):
    @pl.when(pl.program_id(0) == 0)
    def _():
        down_ref[...] = jnp.zeros_like(down_ref)

    permuted = jnp.concatenate([p[...] for p in (p0, p1, p2, p3)], axis=0)
    out_ref[...] = (mixer_ref[...].astype(F32) + tn(wd_ref[...], permuted)).astype(BF16)
    down_ref[...] += nt(permuted, cot_ref[...])


def output_part(mixer, parts, cotangent, wd):
    cols = pl.BlockSpec((64, 4096), lambda i: (0, i))
    part = pl.BlockSpec((32, 4096), lambda i: (0, i))
    return pl.pallas_call(
        output_kernel,
        grid=(4,),
        in_specs=[cols] + [part] * 4 + [cols, full(wd.shape)],
        out_specs=[cols, full((128, 64))],
        out_shape=[jax.ShapeDtypeStruct(mixer.shape, BF16), jax.ShapeDtypeStruct((128, 64), F32)],
        compiler_params=params(60),
        cost_estimate=cost(8),
        name="output_part",
    )(mixer, *parts, cotangent, wd)


def swap(values, axis, bit):
    size = int(np.prod([SIZES[AXES.index(a)] for a in ((axis,) if isinstance(axis, str) else axis)]))
    return lax.ppermute(values, axis, [(i, i ^ bit) for i in range(size)])


def chan_swap(parts):
    return [parts[0]] + [swap(parts[i], CHAN, i) for i in (1, 2, 3)]


def start_gather(first, second, core, after):
    both = jnp.stack([first, second]).reshape(2, 4, 2, 512)
    mine = lax.dynamic_index_in_dim(both, core, 2, keepdims=False)
    theirs = lax.dynamic_index_in_dim(both, 1 - core, 2, keepdims=False)
    theirs = swap(theirs, "core", 1)
    rows = jnp.where(
        core == 0,
        jnp.concatenate([mine, theirs], axis=1),
        jnp.concatenate([theirs, mine], axis=1),
    )
    column = lax.all_to_all(fan(fan_kernel, rows, (8,) + rows.shape, after), "z", 0, 0, tiled=True)
    return column


def local(tokens, gate_in, gate_out, twiddle, first_factor, second_factor, w_up, w_down, cotangent):
    core = lax.axis_index("core")
    chan = lax.axis_index(CHAN)
    order = chan ^ jnp.arange(4, dtype=jnp.int32)
    table = jnp.concatenate([jnp.arange(16, dtype=jnp.int32), core.astype(jnp.int32).reshape(1)])
    wd = w_down[0].reshape(4, 32, 64)[order].reshape(128, 64)
    wu = w_up[0].reshape(64, 4, 32)[:, order].reshape(64, 128)

    second_turned = jnp.swapaxes(second_factor.reshape(4, 64, 16), 1, 2).reshape(4, 1024)
    grads = grads_part(cotangent, wd)
    column = start_gather(first_factor, second_turned, core, [grads[0]])
    rows = gated_part(tokens, gate_in)
    grads = chan_swap(grads)
    plane = lax.all_to_all(
        fan(fan_plane_kernel, column, (16, 2, 8, 8, 512), [grads[1], grads[2], rows]), PLANE, 0, 0, tiled=True
    )
    first = assemble(plane, swap(plane[:, 0], "core", 1), table, 0)
    seg = segment(first, rows, twiddle)
    moved = lax.all_to_all(seg.reshape(64, 16, 1024), SEQ, 0, 0, tiled=True).reshape(1024, 1024)
    second = assemble(plane, swap(plane[:, 1], "core", 1), table, 1)
    back, left, weighted, mixer, *rest = middle(moved, second, gate_out, cotangent, grads, wu)
    acts, up = rest[:4], rest[4]
    returned = lax.all_to_all(back.reshape(64, 16, 1024), SEQ, 0, 0, tiled=True).reshape(1024, 1024)
    acts = chan_swap(acts)
    second_send, second_keep = second_part(table, weighted, left)
    second_got = swap(second_send, "core", 1)
    mixed_out, down = output_part(mixer, acts, cotangent, wd)
    up = up.reshape(64, 4, 32)[:, order].reshape(64, 128)
    down = down.reshape(4, 32, 64)[order].reshape(128, 64)
    small = jnp.concatenate([up.reshape(16, 512), down.reshape(16, 512)], axis=0)
    first_send, first_keep, shifted = first_part(
        table, returned, rows, twiddle, [down, second_got]
    )
    small = (small + swap(small, "x", 1)) + (swap(small, "x", 2) + swap(small, "x", 3))
    joined = join(first_keep, swap(first_send, "core", 1), second_keep, second_got)
    parts = lax.all_to_all(joined, PLANE, 0, 0, tiled=True)
    small = small + swap(small, "yh", 1)
    both = plane_sum(parts, small)
    input_grad, done = input_part(shifted, first, gate_in, both)
    both = lax.all_to_all(both, "z", 0, 0, tiled=True)
    both = z_sum(both, done)
    small = both[2:].reshape(32, 512)
    both = both[:2].reshape(2, 2, 4, 512)
    mine = lax.dynamic_index_in_dim(both, core, 1, keepdims=False)
    theirs = swap(lax.dynamic_index_in_dim(both, 1 - core, 1, keepdims=False), "core", 1)
    both = jnp.where(
        core == 0,
        jnp.concatenate([mine, theirs], axis=2),
        jnp.concatenate([theirs, mine], axis=2),
    )
    return (
        mixed_out,
        input_grad,
        both[0],
        jnp.swapaxes(both[1].reshape(4, 16, 64), 1, 2).reshape(4, 1024),
        small[:16].reshape(1, 64, 128),
        small[16:].reshape(1, 128, 64),
    )


def solution(mesh):
    fine = Mesh(mesh.devices.reshape(SIZES), AXES)
    wide = P(CHAN, SEQ)
    factor = P(AXES, None)
    weight = P(CHAN, None, None)
    return jax.shard_map(
        local,
        mesh=fine,
        in_specs=(wide, wide, wide, P(SEQ, None), factor, factor, weight, weight, wide),
        out_specs=(wide, wide, factor, factor, weight, weight),
        check_vma=False,
    )
```

```python
import functools

import jax
import jax.numpy as jnp
import numpy as np
from jax import lax
from jax.experimental import pallas as pl
from jax.experimental.pallas import tpu as pltpu
from jax.sharding import Mesh
from jax.sharding import PartitionSpec as P

AXES = ("z", "yh", "x", "yl", "core")
SIZES = (8, 2, 4, 2, 2)
SEQ = ("z", "yh", "x")
CHAN = ("yl", "core")
PLANE = ("yh", "x", "yl")
F32 = jnp.float32
BF16 = jnp.bfloat16
MIB = 1024 * 1024


def params(mib, **kw):
    return pltpu.CompilerParams(vmem_limit_bytes=mib * MIB, **kw)


def cost(us, flops=0):
    return pl.CostEstimate(flops=flops, bytes_accessed=int(us * 3.0e3), transcendentals=0)


def full(shape):
    return pl.BlockSpec(shape, lambda i: (0,) * len(shape))


def nt(a, b):
    return lax.dot_general(a, b, (((1,), (1,)), ((), ())), preferred_element_type=F32)


def nn(a, b):
    return lax.dot_general(a, b, (((1,), (0,)), ((), ())), preferred_element_type=F32)


def tn(a, b):
    return lax.dot_general(a, b, (((0,), (0,)), ((), ())), preferred_element_type=F32)


def grads_kernel(cot_ref, wd_ref, *grad_refs):
    grad = nn(wd_ref[...], cot_ref[...]).astype(BF16)
    for i, ref in enumerate(grad_refs):
        ref[...] = grad[i * 32 : (i + 1) * 32]


def grads_part(cotangent, wd):
    chan, positions = cotangent.shape
    part = pl.BlockSpec((32, 4096), lambda i: (0, i))
    return pl.pallas_call(
        grads_kernel,
        grid=(positions // 4096,),
        in_specs=[pl.BlockSpec((chan, 4096), lambda i: (0, i)), full(wd.shape)],
        out_specs=[part] * 4,
        out_shape=[jax.ShapeDtypeStruct((32, positions), BF16)] * 4,
        compiler_params=params(60),
        cost_estimate=cost(4),
        name="grads_part",
    )(cotangent, wd)


def gated_kernel(tok_ref, gate_ref, rows_ref):
    for q in range(4):
        at = slice(q * 1024, (q + 1) * 1024)
        rows_ref[q * 64 : (q + 1) * 64] = (
            tok_ref[:, at].astype(F32) * gate_ref[:, at].astype(F32)
        ).astype(BF16)


def gated_part(tokens, gate_in):
    cols = pl.BlockSpec((64, 4096), lambda i: (0, i))
    return pl.pallas_call(
        gated_kernel,
        grid=(4,),
        in_specs=[cols, cols],
        out_specs=pl.BlockSpec((256, 1024), lambda i: (i, 0)),
        out_shape=pltpu.HBM((1024, 1024), BF16),
        compiler_params=params(60),
        cost_estimate=cost(4),
        name="gated_part",
    )(tokens, gate_in)


def assemble_kernel(factor, table_ref, own_ref, other_ref, out_ref):
    first = table_ref[16] == 0
    for m in range(16):
        at = table_ref[m]
        own, other = own_ref[at, factor], other_ref[at]
        out_ref[:, m, :, :512] = jnp.where(first, own, other)
        out_ref[:, m, :, 512:] = jnp.where(first, other, own)


def assemble(own, other, table, factor):
    out = pl.pallas_call(
        functools.partial(assemble_kernel, factor),
        in_specs=[pl.BlockSpec(memory_space=pltpu.SMEM)] + [pl.BlockSpec(memory_space=pltpu.VMEM)] * 2,
        out_specs=pl.BlockSpec(memory_space=pltpu.VMEM),
        out_shape=jax.ShapeDtypeStruct((8, 16, 8, 1024), BF16),
        compiler_params=params(12),
        cost_estimate=cost(3),
        name="assemble",
    )(table, own, other)
    return out.reshape(1024, 1024)


def fan_kernel(column_ref, *refs):
    for m in range(refs[-1].shape[0]):
        refs[-1][m] = column_ref[...]


def fan_plane_kernel(column_ref, *refs):
    for m in range(16):
        for z in range(8):
            for factor in range(2):
                refs[-1][m, factor, z] = column_ref[z, factor]


def fan(kernel, column, shape, after):
    vmem = pl.BlockSpec(memory_space=pltpu.VMEM)
    return pl.pallas_call(
        kernel,
        in_specs=[vmem] + [pl.BlockSpec(memory_space=pl.ANY)] * len(after),
        out_specs=vmem,
        out_shape=pltpu.HBM(shape, BF16),
        compiler_params=params(10),
        cost_estimate=cost(1),
        name="fan",
    )(column, *after)


def spread_twiddle(tw):
    high = tw.astype(BF16)
    rest = tw - high.astype(F32)
    mid = rest.astype(BF16)
    low = (rest - mid.astype(F32)).astype(BF16)
    terms = jnp.concatenate([high, mid, low], axis=0)
    row = lax.broadcasted_iota(jnp.int32, (48, 1024), 0)
    lane = lax.broadcasted_iota(jnp.int32, (48, 1024), 1)
    pick = jnp.where(row % 16 == lane // 64, 1.0, 0.0).astype(BF16)
    return tn(terms, pick)


def segment_kernel(first_ref, rows_ref, tw_ref, out_ref):
    scale = spread_twiddle(tw_ref[...])
    out_ref[...] = (nt(first_ref[...], rows_ref[...]) * scale).astype(BF16)


def segment(first, rows, tw):
    return pl.pallas_call(
        segment_kernel,
        grid=(4,),
        in_specs=[
            pl.BlockSpec((256, 1024), lambda i: (i, 0)),
            full((1024, 1024)),
            pl.BlockSpec((16, 256), lambda i: (0, i)),
        ],
        out_specs=pl.BlockSpec((256, 1024), lambda i: (i, 0)),
        out_shape=pltpu.HBM((1024, 1024), BF16),
        compiler_params=params(24),
        cost_estimate=cost(6),
        name="segment",
    )(first, rows, tw)


def swap_lanes(values):
    return pltpu.roll(values, 64, 1)


def middle_kernel(
    moved_ref, second_ref, gate_ref, cot_ref, g0, g1, g2, g3, wu_ref,
    back_ref, left_ref, weighted_ref, mixer_ref, a0, a1, a2, a3, up_ref,
    wide_ref, prod_ref,
):
    step = pl.program_id(0)
    grads, acts = (g0, g1, g2, g3), (a0, a1, a2, a3)

    @pl.when(step == 0)
    def _():
        for p in range(8):
            wide_ref[p * 1024 : (p + 1) * 1024] = moved_ref[:, p * 128 : (p + 1) * 128].astype(F32)
        up_ref[...] = jnp.zeros_like(up_ref)

    low = lax.broadcasted_iota(jnp.int32, (64, 128), 1) < 64
    for pair in range(2):
        k = step * 4 + pair * 2
        for p in range(8):
            lanes = slice(p * 128, (p + 1) * 128)
            one = wide_ref[pl.ds(p * 1024 + k, 64, stride=16)]
            two = wide_ref[pl.ds(p * 1024 + k + 1, 64, stride=16)]
            both = jnp.concatenate(
                [jnp.where(low, one, swap_lanes(two)), jnp.where(low, swap_lanes(one), two)], axis=0
            )
            left_ref[pair * 128 : (pair + 1) * 128, lanes] = both.T.astype(BF16)
    prod_ref[...] = nt(left_ref[...], second_ref[...])
    wu = wu_ref[...]
    up = jnp.zeros((64, 128), F32)
    for unit in range(0, 4, 4):
        at = slice(unit * 1024, (unit + 4) * 1024)
        for kk in range(unit, unit + 4):
            cols = slice(kk * 1024, (kk + 1) * 1024)
            gate = gate_ref[:, cols].astype(F32)
            mixer_ref[:, cols] = (prod_ref[kk * 64 : (kk + 1) * 64] * gate).astype(BF16)
        mix = mixer_ref[:, at]
        hidden = tn(wu, mix)
        cum = 0.5 * (1.0 + lax.erf(hidden * 0.7071067811865476))
        act = (hidden * cum).astype(BF16)
        slope = cum + hidden * (jnp.exp(-0.5 * hidden * hidden) * 0.3989422804014327)
        for i in range(4):
            acts[i][:, at] = act[i * 32 : (i + 1) * 32]
        grad = jnp.concatenate([g[:, at] for g in grads], axis=0)
        hgrad = (grad.astype(F32) * slope).astype(BF16)
        up += nt(mix, hgrad)
        mgrad = nn(wu, hgrad)
        for kk in range(unit, unit + 4):
            cols = slice(kk * 1024, (kk + 1) * 1024)
            total = cot_ref[:, cols].astype(F32) + mgrad[:, (kk - unit) * 1024 : (kk - unit + 1) * 1024]
            weighted_ref[kk * 64 : (kk + 1) * 64] = (total * gate_ref[:, cols].astype(F32)).astype(BF16)
    up_ref[...] += up
    prod_ref[...] = nn(weighted_ref[...], second_ref[...])
    for pair in range(2):
        k = step * 4 + pair * 2
        for p in range(8):
            lanes = slice(p * 128, (p + 1) * 128)
            both = prod_ref[pair * 128 : (pair + 1) * 128, lanes].T
            top, bottom = both[:64], both[64:]
            wide_ref[pl.ds(p * 1024 + k, 64, stride=16)] = jnp.where(low, top, swap_lanes(bottom))
            wide_ref[pl.ds(p * 1024 + k + 1, 64, stride=16)] = jnp.where(low, swap_lanes(top), bottom)

    @pl.when(step == 3)
    def _():
        for p in range(8):
            back_ref[:, p * 128 : (p + 1) * 128] = wide_ref[p * 1024 : (p + 1) * 1024].astype(BF16)


def middle(moved, second, gate_out, cotangent, grads, wu):
    chan, positions = gate_out.shape
    cols = pl.BlockSpec((chan, 4096), lambda i: (0, i))
    part = pl.BlockSpec((32, 4096), lambda i: (0, i))
    square = full((1024, 1024))
    rows = pl.BlockSpec((256, 1024), lambda i: (i, 0))
    big = pltpu.HBM((1024, 1024), BF16)
    small = pltpu.HBM((32, positions), BF16)
    return pl.pallas_call(
        middle_kernel,
        grid=(4,),
        in_specs=[square, square, cols, cols] + [part] * 4 + [full(wu.shape)],
        out_specs=[square, rows, rows, cols] + [part] * 4 + [full((64, 128))],
        out_shape=[big, big, big, pltpu.HBM((chan, positions), BF16)]
        + [small] * 4
        + [jax.ShapeDtypeStruct((64, 128), F32)],
        scratch_shapes=[pltpu.VMEM((8192, 128), F32), pltpu.VMEM((256, 1024), F32)],
        compiler_params=params(44),
        cost_estimate=cost(25),
        name="middle",
    )(moved, second, gate_out, cotangent, *grads, wu)


def split_columns(table_ref, total, send_ref, keep_ref):
    first = table_ref[16] == 0
    for m in range(16):
        at = table_ref[m]
        for z in range(8):
            row = z * 128 + m * 8
            lo, hi = total[row : row + 8, :512], total[row : row + 8, 512:]
            send_ref[at, z] = jnp.where(first, hi, lo).astype(BF16)
            keep_ref[at, z] = jnp.where(first, lo, hi)


def second_kernel(table_ref, weighted_ref, left_ref, send_ref, keep_ref, total_ref):
    total_ref[...] = tn(weighted_ref[...], left_ref[...])
    split_columns(table_ref, total_ref, send_ref, keep_ref)


HALF = [
    jax.ShapeDtypeStruct((16, 8, 8, 512), BF16),
    jax.ShapeDtypeStruct((16, 8, 8, 512), F32),
]


def second_part(table, weighted, left):
    vmem = pl.BlockSpec(memory_space=pltpu.VMEM)
    return pl.pallas_call(
        second_kernel,
        in_specs=[pl.BlockSpec(memory_space=pltpu.SMEM), vmem, vmem],
        out_specs=[vmem, vmem],
        out_shape=HALF,
        scratch_shapes=[pltpu.VMEM((1024, 1024), F32)],
        compiler_params=params(28),
        cost_estimate=cost(7),
        name="second_part",
    )(table, weighted, left)


def first_kernel(table_ref, back_ref, rows_ref, tw_ref, *refs):
    send_ref, keep_ref, shifted_ref, total_ref = refs[-4:]
    for i in range(4):
        at = slice(i * 256, (i + 1) * 256)
        scale = spread_twiddle(tw_ref[:, at])
        shifted_ref[at] = (back_ref[at].astype(F32) * scale).astype(BF16)
    total_ref[...] = nn(shifted_ref[...], rows_ref[...])
    split_columns(table_ref, total_ref, send_ref, keep_ref)


def first_part(table, back, rows, tw, after):
    vmem = pl.BlockSpec(memory_space=pltpu.VMEM)
    return pl.pallas_call(
        first_kernel,
        in_specs=[pl.BlockSpec(memory_space=pltpu.SMEM), vmem, vmem, vmem]
        + [pl.BlockSpec(memory_space=pl.ANY)] * len(after),
        out_specs=[vmem, vmem, vmem],
        out_shape=HALF + [pltpu.HBM((1024, 1024), BF16)],
        scratch_shapes=[pltpu.VMEM((1024, 1024), F32)],
        compiler_params=params(28),
        cost_estimate=cost(7),
        name="first_part",
    )(table, back, rows, tw, *after)


def join_kernel(keep_ref, got_ref, second_keep_ref, second_got_ref, out_ref):
    for m in range(16):
        out_ref[m, 0] = (keep_ref[m] + got_ref[m].astype(F32)).astype(BF16)
        out_ref[m, 1] = (second_keep_ref[m] + second_got_ref[m].astype(F32)).astype(BF16)


def join(keep, got, second_keep, second_got):
    vmem = pl.BlockSpec(memory_space=pltpu.VMEM)
    return pl.pallas_call(
        join_kernel,
        in_specs=[vmem] * 4,
        out_specs=vmem,
        out_shape=pltpu.HBM((16, 2, 8, 8, 512), BF16),
        compiler_params=params(20),
        cost_estimate=cost(3),
        name="join",
    )(keep, got, second_keep, second_got)


def plane_sum_kernel(parts_ref, small_ref, out_ref):
    small = small_ref[...].astype(BF16)
    for z in range(8):
        for grad in range(2):
            total = parts_ref[0, grad, z].astype(F32)
            for m in range(1, 16):
                total += parts_ref[m, grad, z].astype(F32)
            out_ref[z, grad] = total.astype(BF16)
        for i in range(4):
            out_ref[z, 2 + i] = small[i * 8 : (i + 1) * 8]


def plane_sum(parts, small):
    vmem = pl.BlockSpec(memory_space=pltpu.VMEM)
    return pl.pallas_call(
        plane_sum_kernel,
        in_specs=[vmem, vmem],
        out_specs=vmem,
        out_shape=jax.ShapeDtypeStruct((8, 6, 8, 512), BF16),
        compiler_params=params(12),
        cost_estimate=cost(2),
        name="plane_sum",
    )(parts, small)


def z_sum_kernel(parts_ref, after_ref, out_ref):
    total = parts_ref[0].astype(F32)
    for z in range(1, 8):
        total += parts_ref[z].astype(F32)
    out_ref[...] = total


def z_sum(parts, after):
    vmem = pl.BlockSpec(memory_space=pltpu.VMEM)
    return pl.pallas_call(
        z_sum_kernel,
        in_specs=[vmem, pl.BlockSpec(memory_space=pl.ANY)],
        out_specs=vmem,
        out_shape=jax.ShapeDtypeStruct(parts.shape[1:], F32),
        compiler_params=params(10),
        cost_estimate=cost(1),
        name="z_sum",
    )(parts, after)


def input_kernel(shifted_ref, first_ref, gate_ref, after_ref, out_ref, done_ref):
    done_ref[...] = jnp.zeros_like(done_ref)
    spread = tn(shifted_ref[...], first_ref[...])
    for q in range(4):
        at = slice(q * 1024, (q + 1) * 1024)
        out_ref[:, at] = (spread[q * 64 : (q + 1) * 64] * gate_ref[:, at].astype(F32)).astype(BF16)


def input_part(shifted, first, gate_in, after):
    cols = pl.BlockSpec((64, 4096), lambda i: (0, i))
    return pl.pallas_call(
        input_kernel,
        grid=(4,),
        in_specs=[
            pl.BlockSpec((1024, 256), lambda i: (0, i)),
            full((1024, 1024)),
            cols,
            pl.BlockSpec(memory_space=pl.ANY),
        ],
        out_specs=[cols, full((8, 128))],
        out_shape=[
            jax.ShapeDtypeStruct(gate_in.shape, BF16),
            jax.ShapeDtypeStruct((8, 128), F32),
        ],
        compiler_params=params(60),
        cost_estimate=cost(7),
        name="input_part",
    )(shifted, first, gate_in, after)


def output_kernel(mixer_ref, p0, p1, p2, p3, cot_ref, wd_ref, after_ref, out_ref, down_ref):
    @pl.when(pl.program_id(0) == 0)
    def _():
        down_ref[...] = jnp.zeros_like(down_ref)

    permuted = jnp.concatenate([p[...] for p in (p0, p1, p2, p3)], axis=0)
    out_ref[...] = (mixer_ref[...].astype(F32) + tn(wd_ref[...], permuted)).astype(BF16)
    down_ref[...] += nt(permuted, cot_ref[...])


def output_part(mixer, parts, cotangent, wd, after):
    cols = pl.BlockSpec((64, 4096), lambda i: (0, i))
    part = pl.BlockSpec((32, 4096), lambda i: (0, i))
    return pl.pallas_call(
        output_kernel,
        grid=(4,),
        in_specs=[cols] + [part] * 4 + [cols, full(wd.shape), pl.BlockSpec(memory_space=pl.ANY)],
        out_specs=[cols, full((128, 64))],
        out_shape=[jax.ShapeDtypeStruct(mixer.shape, BF16), jax.ShapeDtypeStruct((128, 64), F32)],
        compiler_params=params(60),
        cost_estimate=cost(8),
        name="output_part",
    )(mixer, *parts, cotangent, wd, after)


def swap(values, axis, bit):
    size = int(np.prod([SIZES[AXES.index(a)] for a in ((axis,) if isinstance(axis, str) else axis)]))
    return lax.ppermute(values, axis, [(i, i ^ bit) for i in range(size)])


def chan_swap(parts):
    return [parts[0]] + [swap(parts[i], CHAN, i) for i in (1, 2, 3)]


def start_gather(first, second, core, after):
    both = jnp.stack([first, second]).reshape(2, 4, 2, 512)
    mine = lax.dynamic_index_in_dim(both, core, 2, keepdims=False)
    theirs = lax.dynamic_index_in_dim(both, 1 - core, 2, keepdims=False)
    theirs = swap(theirs, "core", 1)
    rows = jnp.where(
        core == 0,
        jnp.concatenate([mine, theirs], axis=1),
        jnp.concatenate([theirs, mine], axis=1),
    )
    column = lax.all_to_all(fan(fan_kernel, rows, (8,) + rows.shape, after), "z", 0, 0, tiled=True)
    return column


def local(tokens, gate_in, gate_out, twiddle, first_factor, second_factor, w_up, w_down, cotangent):
    core = lax.axis_index("core")
    chan = lax.axis_index(CHAN)
    order = chan ^ jnp.arange(4, dtype=jnp.int32)
    table = jnp.concatenate([jnp.arange(16, dtype=jnp.int32), core.astype(jnp.int32).reshape(1)])
    wd = w_down[0].reshape(4, 32, 64)[order].reshape(128, 64)
    wu = w_up[0].reshape(64, 4, 32)[:, order].reshape(64, 128)

    second_turned = jnp.swapaxes(second_factor.reshape(4, 64, 16), 1, 2).reshape(4, 1024)
    grads = grads_part(cotangent, wd)
    column = start_gather(first_factor, second_turned, core, [grads[0]])
    rows = gated_part(tokens, gate_in)
    grads = chan_swap(grads)
    plane = lax.all_to_all(
        fan(fan_plane_kernel, column, (16, 2, 8, 8, 512), [grads[1], grads[2], rows]), PLANE, 0, 0, tiled=True
    )
    first = assemble(plane, swap(plane[:, 0], "core", 1), table, 0)
    seg = segment(first, rows, twiddle)
    moved = lax.all_to_all(seg.reshape(64, 16, 1024), SEQ, 0, 0, tiled=True).reshape(1024, 1024)
    second = assemble(plane, swap(plane[:, 1], "core", 1), table, 1)
    back, left, weighted, mixer, *rest = middle(moved, second, gate_out, cotangent, grads, wu)
    acts, up = rest[:4], rest[4]
    returned = lax.all_to_all(back.reshape(64, 16, 1024), SEQ, 0, 0, tiled=True).reshape(1024, 1024)
    acts = chan_swap(acts)
    second_send, second_keep = second_part(table, weighted, left)
    second_got = swap(second_send, "core", 1)
    first_send, first_keep, shifted = first_part(
        table, returned, rows, twiddle, [acts[1], acts[2], acts[3], second_got]
    )
    joined = join(first_keep, swap(first_send, "core", 1), second_keep, second_got)
    parts = lax.all_to_all(joined, PLANE, 0, 0, tiled=True)
    mixed_out, down = output_part(mixer, acts, cotangent, wd, joined)
    up = up.reshape(64, 4, 32)[:, order].reshape(64, 128)
    down = down.reshape(4, 32, 64)[order].reshape(128, 64)
    small = jnp.concatenate([up.reshape(16, 512), down.reshape(16, 512)], axis=0)
    small = (small + swap(small, "x", 1)) + (swap(small, "x", 2) + swap(small, "x", 3))
    small = small + swap(small, "yh", 1)
    both = plane_sum(parts, small)
    input_grad, done = input_part(shifted, first, gate_in, both)
    both = lax.all_to_all(both, "z", 0, 0, tiled=True)
    both = z_sum(both, done)
    small = both[2:].reshape(32, 512)
    both = both[:2].reshape(2, 2, 4, 512)
    mine = lax.dynamic_index_in_dim(both, core, 1, keepdims=False)
    theirs = swap(lax.dynamic_index_in_dim(both, 1 - core, 1, keepdims=False), "core", 1)
    both = jnp.where(
        core == 0,
        jnp.concatenate([mine, theirs], axis=2),
        jnp.concatenate([theirs, mine], axis=2),
    )
    return (
        mixed_out,
        input_grad,
        both[0],
        jnp.swapaxes(both[1].reshape(4, 16, 64), 1, 2).reshape(4, 1024),
        small[:16].reshape(1, 64, 128),
        small[16:].reshape(1, 128, 64),
    )


def solution(mesh):
    fine = Mesh(mesh.devices.reshape(SIZES), AXES)
    wide = P(CHAN, SEQ)
    factor = P(AXES, None)
    weight = P(CHAN, None, None)
    return jax.shard_map(
        local,
        mesh=fine,
        in_specs=(wide, wide, wide, P(SEQ, None), factor, factor, weight, weight, wide),
        out_specs=(wide, wide, factor, factor, weight, weight),
        check_vma=False,
    )
```
